128 devices in a mesh: group: 8 (over z, core), member: 16 (over x, y).
Axes of the slice: x: 4, y: 4, z: 4, core: 2. Of those that a mesh axis runs over, the one named last changes fastest.
Arguments:
- query_feat: bfloat16 [16384, 4096], P(('group', 'member'))
- code_feat: bfloat16 [16384, 4096], P(('group', 'member'))
- projection: bfloat16 [4096, 1024], replicated
- hard_ids: int32 [128, 16], P(('group', 'member')), may hold values from 0 to 255, as said below
- loss_weight: float32 [16384], P(('group', 'member')), may hold values from 1 to 4
Outputs:
- query_grad: bfloat16 [16384, 4096], P(('group', 'member'))
- code_grad: bfloat16 [16384, 4096], P(('group', 'member'))
- projection_grad: float32 [4096, 1024], P(('group', 'member'))
The draws below stay inside these ranges and needn't reach their ends.
Inputs may be any that keep to these rules, and one draw needn't show every extreme that they name: `hard_ids`: entry (owner device g * 16 + m) * 2 + slot names code rows of that device. A row names 16 different blocks, none of its own group; at most 4 of them lie in one group, and exactly 4 in some group of every row.
All inputs are finite; a program needn't handle non-finite values.
Results may differ from the reference program's by a relative error of at most 0.02.
Values may be sent and summed in bfloat16 or wider, within the bound.
A program may use at most 128 MiB of HBM per device.

```python
import math
import jax
import jax.numpy as jnp
from jax import lax

D = 4096
E = 1024
QB = 128
CB = 64
HARD = 16
CAP = 4
PAIRS = 16384
N_GROUP = 8
N_MEMBER = 16


def row_scales(key):
    return jnp.exp(jax.random.uniform(key, (PAIRS, 1), jnp.float32, math.log(0.2), math.log(2.0)))


def code_features(key):
    array_shape = (PAIRS, D)
    scales = row_scales(jax.random.fold_in(key, 102))
    values = jax.random.normal(jax.random.fold_in(key, 101), array_shape, jnp.float32)
    return values * scales


def draw_code_feat(key, part):
    return code_features(key).astype(jnp.bfloat16)


def draw_query_feat(key, part):
    array_shape = (PAIRS, D)
    scales = row_scales(jax.random.fold_in(key, 202))
    values = jax.random.normal(jax.random.fold_in(key, 201), array_shape, jnp.float32) * scales
    return values.astype(jnp.bfloat16)


def draw_projection(key, part):
    values = jax.random.normal(jax.random.fold_in(key, 302), (D, E), jnp.float32)
    column_scale = jnp.exp(jax.random.uniform(jax.random.fold_in(key, 301), (1, E), jnp.float32, math.log(4.0), math.log(40.0)))
    return (values * column_scale * D ** (-0.5)).astype(jnp.bfloat16)


def draw_hard_ids(key, part):
    devices = N_GROUP * N_MEMBER
    per_group = N_MEMBER * (QB // CB)
    others = N_GROUP - 1
    spill_count = HARD - CAP

    def one_row(row_key, device):
        row_keys = jax.random.split(row_key, 4)
        chosen = jax.random.permutation(row_keys[0], (others - 1) * CAP)[:spill_count].astype(jnp.int32)
        rank_of = jnp.concatenate([jnp.zeros((CAP,), jnp.int32), 1 + chosen // CAP])
        places = jnp.concatenate([jnp.arange(CAP, dtype=jnp.int32), chosen % CAP])
        shuffle_groups = jax.random.permutation(row_keys[1], others).astype(jnp.int32)
        target = (device // N_MEMBER + 1 + shuffle_groups[rank_of]) % N_GROUP
        within = jax.vmap(lambda subkey: jax.random.permutation(subkey, per_group))(jax.random.split(row_keys[2], others)).astype(jnp.int32)
        local_block = within[rank_of, places]
        entries = (target * per_group + local_block).astype(jnp.int32)
        return entries[jax.random.permutation(row_keys[3], HARD)]
    return jax.vmap(one_row)(jax.random.split(key, devices), jnp.arange(devices, dtype=jnp.int32))


def shard_levels(own_key, shape, shards, smallest, largest):
    loudness, own = 1.0, jax.random.fold_in(own_key, 6)
    for dim, parts in shards:
        draws = jnp.exp(jax.random.uniform(jax.random.fold_in(own, dim), (parts,), jnp.float32, smallest / len(shards), largest / len(shards)))
        loudness = loudness * jnp.repeat(draws, shape[dim] // parts).reshape([-1 if axis == dim else 1 for axis in range(len(shape))])
    return loudness


def setup_inputs(seed: int = 0) -> dict:
    seeds = jax.random.split(jax.random.key(seed), 6)
    query_feat = draw_query_feat(jax.random.fold_in(seeds[5], 71), 0)
    code_feat = draw_code_feat(jax.random.fold_in(seeds[5], 71), 0)
    projection = draw_projection(jax.random.fold_in(seeds[5], 71), 0)
    hard_ids = draw_hard_ids(jax.random.fold_in(seeds[5], 71), 0)
    loss_weight = jnp.clip(jnp.exp(math.log(4.0) - 1.3862944 * jax.random.uniform(seeds[4], (PAIRS,), jnp.float32) ** shard_levels(seeds[4], (PAIRS,), ((0, 128),), -0.2, 0.2)), 1.0, 4.0)
    return dict(query_feat=query_feat, code_feat=code_feat, projection=projection, hard_ids=hard_ids, loss_weight=loss_weight)


inverse_temp = 120.0
epsilon = 1e-06

def embed(features, projection):
    values = jnp.dot(features, projection, preferred_element_type=jnp.float32)
    inverse = lax.rsqrt(lax.optimization_barrier(jnp.sum(values * values, axis=1)) + epsilon)
    unit_vec = values * inverse[:, None]
    return (unit_vec, inverse, unit_vec.astype(jnp.bfloat16))

def norm_back(upstream, unit_vec, inverse):
    inner_prod = lax.optimization_barrier(jnp.sum(unit_vec * upstream, axis=1, keepdims=True))
    return (inverse[:, None] * (upstream - unit_vec * inner_prod)).astype(jnp.bfloat16)

def reference(query_feat, code_feat, projection, hard_ids, loss_weight):
    devices = N_GROUP * N_MEMBER
    slot_count = QB // CB
    group_span = N_MEMBER * QB
    q_unit, q_inv, q_emb = embed(query_feat, projection)
    c_unit, c_inv, c_emb = embed(code_feat, projection)
    code_blocks = c_emb.reshape(devices * slot_count, CB, E)
    offsets = jnp.arange(QB, dtype=jnp.int32)
    columns = jnp.arange(group_span, dtype=jnp.int32)

    def one_block(carry, device):
        group_index = device // N_MEMBER
        member_index = device % N_MEMBER
        queries = lax.dynamic_slice_in_dim(q_emb, device * QB, QB, 0)
        weights = lax.dynamic_slice_in_dim(loss_weight, device * QB, QB, 0)
        first_row = group_index * group_span
        in_group = lax.dynamic_slice_in_dim(c_emb, first_row, group_span, 0)
        wanted = lax.dynamic_index_in_dim(hard_ids, device, 0, keepdims=False)
        negatives = code_blocks[wanted].reshape(HARD * CB, E)
        group_scores = inverse_temp * jnp.dot(queries, in_group.T, preferred_element_type=jnp.float32)
        hard_scores = inverse_temp * jnp.dot(queries, negatives.T, preferred_element_type=jnp.float32)
        row_max = jnp.maximum(lax.optimization_barrier(jnp.max(group_scores, axis=1)), lax.optimization_barrier(jnp.max(hard_scores, axis=1)))
        row_sum = lax.optimization_barrier(jnp.sum(jnp.exp(group_scores - row_max[:, None]), axis=1)) + lax.optimization_barrier(jnp.sum(jnp.exp(hard_scores - row_max[:, None]), axis=1))
        log_total = row_max + jnp.log(row_sum)
        factor = weights * inverse_temp
        positive = (columns[None, :] == (member_index * QB + offsets)[:, None]).astype(jnp.float32)
        grad_group = (factor[:, None] * (jnp.exp(group_scores - log_total[:, None]) - positive)).astype(jnp.bfloat16)
        grad_hard = (factor[:, None] * jnp.exp(hard_scores - log_total[:, None])).astype(jnp.bfloat16)
        query_delta = jnp.dot(grad_group, in_group, preferred_element_type=jnp.float32) + jnp.dot(grad_hard, negatives, preferred_element_type=jnp.float32)
        group_terms = jnp.dot(grad_group.T, queries, preferred_element_type=jnp.float32)
        hard_terms = lax.optimization_barrier(jnp.dot(grad_hard.T, queries, preferred_element_type=jnp.float32).astype(jnp.bfloat16)).astype(jnp.float32)
        current = lax.dynamic_slice_in_dim(carry, first_row, group_span, 0)
        carry = lax.dynamic_update_slice_in_dim(carry, current + group_terms, first_row, 0)
        blocked = carry.reshape(devices * slot_count, CB, E).at[wanted].add(hard_terms.reshape(HARD, CB, E))
        return (blocked.reshape(devices * QB, E), query_delta)
    code_delta, query_delta = lax.scan(one_block, jnp.zeros((devices * QB, E), jnp.float32), jnp.arange(devices, dtype=jnp.int32))
    query_delta = query_delta.reshape(devices * QB, E)
    dz_query = norm_back(query_delta, q_unit, q_inv)
    dz_code = norm_back(code_delta, c_unit, c_inv)
    query_grad = jnp.dot(dz_query, projection.T, preferred_element_type=jnp.float32).astype(jnp.bfloat16)
    code_grad = jnp.dot(dz_code, projection.T, preferred_element_type=jnp.float32).astype(jnp.bfloat16)
    projection_grad = jnp.dot(query_feat.T, dz_query, preferred_element_type=jnp.float32) + jnp.dot(code_feat.T, dz_code, preferred_element_type=jnp.float32)
    return (query_grad, code_grad, projection_grad)
```

```python
import functools

import jax
import jax.numpy as jnp
from jax import lax
from jax.experimental import pallas as pl
from jax.experimental.pallas import tpu as pltpu
from jax.sharding import PartitionSpec as P

MESH = pl.DeviceIdType.MESH
F32 = jnp.float32
BF16 = jnp.bfloat16
inverse_temp = 120.0
epsilon = 1e-06
LOW = -1e30

PLACE = {2: 0, 1: 1, 3: 2, 0: 3}
LINE = [(dz, dk) for dz in (2, 1, 3, 0) for dk in (0, 1)]
PEERS = [p for p in LINE if p != (0, 0)]


def slot(dz, dk):
    return 2 * PLACE[dz % 4] + dk % 2


OWN = slot(0, 0)


class Links:
    def __init__(self, send, recv):
        self.send, self.recv, self.made = send, recv, []
        group, member = lax.axis_index("group"), lax.axis_index("member")
        self.z, self.core = group // 2, group % 2
        self.x, self.y = member // 4, member % 4

    def device(self, dx=0, dy=0, dz=0, dk=0):
        group = 2 * ((self.z + dz % 4) % 4) + (self.core + dk) % 2
        member = 4 * ((self.x + dx % 4) % 4) + (self.y + dy % 4) % 4
        return (group, member)

    def start(self, src, dst, **where):
        i = len(self.made)
        copy = pltpu.make_async_remote_copy(
            src_ref=src,
            dst_ref=dst,
            send_sem=self.send.at[i],
            recv_sem=self.recv.at[i],
            device_id=self.device(**where),
            device_id_type=MESH,
        )
        copy.start()
        self.made.append(copy)
        return copy

    def barrier(self, places):
        sem = pltpu.get_barrier_semaphore()
        for where in places:
            pl.semaphore_signal(sem, inc=1, device_id=self.device(**where), device_id_type=MESH)
        pl.semaphore_wait(sem, len(places))

    def drain(self):
        for copy in self.made:
            copy.wait_send()


def dot_nt(a, b):
    return lax.dot_general(a, b, (((1,), (1,)), ((), ())), preferred_element_type=F32)


def dot_tn(a, b):
    return lax.dot_general(a, b, (((0,), (0,)), ((), ())), preferred_element_type=F32)


def add_into(dst, *terms):
    total = terms[0].astype(F32)
    for term in terms[1:]:
        total = total + term.astype(F32)
    dst[...] = total.astype(dst.dtype)


def norm_back(upstream, unit, inverse):
    inner = jnp.sum(unit * upstream, axis=1, keepdims=True)
    return (inverse * (upstream - unit * inner)).astype(BF16)


def attend(
    q_ref, c_ref, note_ref, qu_ref, qi_ref, cu_ref, ci_ref, qf_ref, cf_ref,
    dz_ref, half_ref,
    queries, codes, scores, grads, dcode, dquery, notes, mine, stats, top, mass, lse, scale,
    yp0, ym0, yp1, ym1, xp0, xm0, xp1, xm1, sib, zp0, zm0, zp1, zm1, low_a, low_b, dc_sum,
    send, recv, local,
):
    width = q_ref.shape[1]
    link = Links(send, recv)
    link.barrier(
        [dict(dx=1), dict(dx=-1), dict(dy=1), dict(dy=-1)]
        + [dict(dz=dz, dk=dk) for dz, dk in PEERS]
    )

    def q_rows(dz, dk, at=0, n=128):
        return queries.at[pl.ds(128 * slot(dz, dk) + at, n)]

    def code(half, first, second, at=0, n=64):
        return codes.at[pl.ds(256 * (4 * half + second) + 64 * first + at, n)]

    axes = (("dx", "dy"), ("dy", "dx"))

    note_in = {}
    for dz, dk in PEERS:
        s, r = slot(dz, dk), slot(-dz, dk)
        note_in[r] = link.start(note_ref.at[s], notes.at[r], dz=dz, dk=dk)
    codes[0:64] = c_ref[0:64]
    codes[1024:1088] = c_ref[64:128]
    queries[pl.ds(128 * OWN, 128)] = q_ref[...]
    notes[OWN] = note_ref[OWN]
    near = {}
    for h in (0, 1):
        a = axes[h][0]
        near[h, 3] = link.start(code(h, 0, 0), code(h, 3, 0), **{a: 1})
        near[h, 1] = link.start(code(h, 0, 0), code(h, 1, 0), **{a: -1})
    q_in = {}
    q_in[3] = link.start(q_ref, q_rows(3, 0), dz=1)
    q_in[1] = link.start(q_ref, q_rows(1, 0), dz=-1)
    s_in = {0: link.start(q_ref, q_rows(0, 1), dk=1)}

    step = {}

    def spread(h, f):
        b = axes[h][1]
        step[h, f, 3] = link.start(code(h, f, 0), code(h, f, 3), **{b: 1})
        step[h, f, 1] = link.start(code(h, f, 0), code(h, f, 1), **{b: -1})

    far = {}
    for h in (0, 1):
        spread(h, 0)
    for h in (0, 1):
        a = axes[h][0]
        near[h, 1].wait_recv()
        far[h, 0] = link.start(code(h, 1, 0, 0, 32), code(h, 2, 0, 0, 32), **{a: -1})
        spread(h, 1)
        near[h, 3].wait_recv()
        far[h, 1] = link.start(code(h, 3, 0, 32, 32), code(h, 2, 0, 32, 32), **{a: 1})
        spread(h, 3)

    moves, shared = [], []
    for i, f_ref in enumerate((qf_ref, cf_ref)):
        for zz in range(4):
            keep = pl.ds(pl.multiple_of((2 * zz + link.core) * 512, 512), 512)
            give = pl.ds(pl.multiple_of((2 * zz + 1 - link.core) * 512, 512), 512)
            move = pltpu.make_async_copy(
                f_ref.at[:, keep],
                half_ref.at[pl.ds(128 * i, 128), pl.ds(512 * zz, 512)],
                local.at[4 * i + zz],
            )
            move.start()
            moves.append(move)
            shared.append(
                link.start(
                    f_ref.at[:, give],
                    half_ref.at[pl.ds(256 + 128 * i, 128), pl.ds(512 * zz, 512)],
                    dk=1,
                )
            )

    top[...] = jnp.full(top.shape, LOW, F32)
    mass[...] = jnp.zeros(mass.shape, F32)

    q_in[1].wait_recv()
    q_far0 = link.start(q_rows(1, 0, 0, 64), q_rows(2, 0, 0, 64), dz=-1)
    s_in[1] = link.start(q_rows(1, 0), q_rows(1, 1), dk=1)
    q_in[3].wait_recv()
    q_far1 = link.start(q_rows(3, 0, 64, 64), q_rows(2, 0, 64, 64), dz=1)
    s_in[3] = link.start(q_rows(3, 0), q_rows(3, 1), dk=1)
    for h in (0, 1):
        far[h, 0].wait_recv()
        far[h, 1].wait_recv()
        spread(h, 2)

    last = {}

    def onward(f):
        for h in (0, 1):
            b = axes[h][1]
            step[h, f, 1].wait_recv()
            last[h, f, 0] = link.start(code(h, f, 1, 0, 32), code(h, f, 2, 0, 32), **{b: -1})
            step[h, f, 3].wait_recv()
            last[h, f, 1] = link.start(code(h, f, 3, 32, 32), code(h, f, 2, 32, 32), **{b: 1})

    def score(t):
        rows = pl.ds(256 * t, 256)

        def part(j, carry):
            lanes = pl.ds(pl.multiple_of(256 * j, 256), 256)
            s = inverse_temp * dot_nt(codes[rows], queries[pl.ds(pl.multiple_of(256 * j, 256), 256)])
            pieces = []
            for u in range(4):
                bias = jnp.concatenate(
                    [notes[2 * j, 4 * t + u : 4 * t + u + 1], notes[2 * j + 1, 4 * t + u : 4 * t + u + 1]],
                    axis=1,
                )
                pieces.append(s[64 * u : 64 * u + 64] + bias)
            s = jnp.concatenate(pieces, axis=0)
            scores[rows, lanes] = s
            before = top[:, lanes]
            after = jnp.maximum(before, jnp.max(s, axis=0, keepdims=True))
            mass[:, lanes] = mass[:, lanes] * jnp.exp(before - after) + jnp.sum(
                jnp.exp(s - after), axis=0, keepdims=True
            )
            top[:, lanes] = after
            return carry

        lax.fori_loop(0, 4, part, 0)

    onward(0)
    onward(1)
    q_far0.wait_recv()
    q_far1.wait_recv()
    s_in[2] = link.start(q_rows(2, 0), q_rows(2, 1), dk=1)
    onward(3)
    for copy in note_in.values():
        copy.wait_recv()
    for dz in (0, 1, 3, 2):
        s_in[dz].wait_recv()
    score(0)
    score(4)
    onward(2)
    for t in (1, 3, 5, 7):
        score(t)
    for h in (0, 1):
        for f in range(4):
            last[h, f, 0].wait_recv()
            last[h, f, 1].wait_recv()
        score(4 * h + 2)

    for s in range(8):
        mine[s : s + 1] = top[:, 128 * s : 128 * s + 128]
        mine[8 + s : 9 + s] = mass[:, 128 * s : 128 * s + 128]
    told = []
    for dz, dk in PEERS:
        told.append(link.start(mine, stats.at[slot(-dz, dk)], dz=dz, dk=dk))
    stats[OWN] = mine[...]
    for copy in told:
        copy.wait_recv()
    for tz, tk in LINE:
        t = slot(tz, tk)
        seen = [(slot(rz, rk), slot(tz - rz, tk + rk)) for rz, rk in LINE]
        most = functools.reduce(jnp.maximum, [stats[r, i : i + 1] for r, i in seen])
        whole = sum(stats[r, 8 + i : 9 + i] * jnp.exp(stats[r, i : i + 1] - most) for r, i in seen)
        lse[:, 128 * t : 128 * t + 128] = most + jnp.log(whole)
        scale[:, 128 * t : 128 * t + 128] = inverse_temp * notes[t, 32:33]

    def backward(t):
        rows = pl.ds(256 * t, 256)

        def part(j, carry):
            lanes = pl.ds(pl.multiple_of(256 * j, 256), 256)
            grads[rows, lanes] = (
                scale[:, lanes] * jnp.exp(scores[rows, lanes] - lse[:, lanes])
            ).astype(BF16)
            return carry

        lax.fori_loop(0, 4, part, 0)
        if t % 4 == 0:
            lanes = slice(128 * OWN, 128 * OWN + 128)
            own = slice(256 * t, 256 * t + 64)
            i = lax.broadcasted_iota(jnp.int32, (64, 128), 0) + 16 * t
            j = lax.broadcasted_iota(jnp.int32, (64, 128), 1)
            hit = jnp.where(i == j, 1.0, 0.0).astype(F32)
            grads[own, lanes] = (
                scale[:, lanes] * (jnp.exp(scores[own, lanes] - lse[:, lanes]) - hit)
            ).astype(BF16)

        def product(n, carry):
            cols = pl.ds(pl.multiple_of(256 * n, 256), 256)
            dcode[rows, cols] = jnp.dot(
                grads[rows, :], queries[:, cols], preferred_element_type=F32
            ).astype(BF16)
            return carry

        lax.fori_loop(0, width // 256, product, 0)

    def tile(h, t, at, n):
        return dcode.at[pl.ds(256 * (4 * h + t) + at, n)]

    back = {}
    for h in (0, 1):
        b = axes[h][1]
        backward(4 * h + 2)
        back[h, "p0"] = link.start(tile(h, 2, 0, 128), yp0.at[h], **{b: 1})
        back[h, "m0"] = link.start(tile(h, 2, 128, 128), ym0.at[h], **{b: -1})
    for h in (0, 1):
        b = axes[h][1]
        backward(4 * h + 1)
        back[h, "p1"] = link.start(tile(h, 1, 128, 128), yp1.at[h, pl.ds(128, 128)], **{b: 1})
        backward(4 * h + 3)
        back[h, "m1"] = link.start(tile(h, 3, 0, 128), ym1.at[h, pl.ds(0, 128)], **{b: -1})
    for h in (0, 1):
        b = axes[h][1]
        back[h, "p0"].wait_recv()
        add_into(tile(h, 1, 0, 128), tile(h, 1, 0, 128)[...], yp0[h])
        back[h, "p2"] = link.start(tile(h, 1, 0, 128), yp1.at[h, pl.ds(0, 128)], **{b: 1})
        back[h, "m0"].wait_recv()
        add_into(tile(h, 3, 128, 128), tile(h, 3, 128, 128)[...], ym0[h])
        back[h, "m2"] = link.start(tile(h, 3, 128, 128), ym1.at[h, pl.ds(128, 128)], **{b: -1})
    backward(0)
    backward(4)

    home = {}
    for p, dz in enumerate((2, 1, 3, 0)):
        at = pl.ds(256 * p, 256)
        lhs = grads[:, 256 * p : 256 * p + 256]

        def product(n, carry, lhs=lhs, at=at):
            cols = pl.ds(pl.multiple_of(256 * n, 256), 256)
            dquery[at, cols] = dot_tn(lhs, codes[:, cols]).astype(BF16)
            return carry

        lax.fori_loop(0, width // 256, product, 0)
        home[dz] = link.start(dquery.at[pl.ds(256 * p + 128, 128)], sib.at[p], dk=1)

    def dq(dz, at=0, n=128):
        return dquery.at[pl.ds(128 * slot(dz, 0) + at, n)]

    for dz in (2, 1, 3):
        home[dz].wait_recv()
        add_into(dq(dz), dq(dz)[...], sib[PLACE[dz]])
        if dz == 2:
            z0p = link.start(dq(2, 0, 64), zp0, dz=1)
            z0m = link.start(dq(2, 64, 64), zm0, dz=-1)
        elif dz == 1:
            z1p = link.start(dq(1, 64, 64), zp1.at[pl.ds(64, 64)], dz=1)
        else:
            z1m = link.start(dq(3, 0, 64), zm1.at[pl.ds(0, 64)], dz=-1)

    def inner(h):
        a = axes[h][0]
        for name in ("p1", "p2", "m1", "m2"):
            back[h, name].wait_recv()
        low = (low_a, low_b)[h]
        for f in (2, 1, 3, 0):
            s = slice(64 * f, 64 * f + 64)
            total = (
                tile(h, 0, 64 * f, 64)[...].astype(F32)
                + yp1[h, s].astype(F32)
                + ym1[h, s].astype(F32)
            )
            if f == 0:
                dc_sum[64 * h : 64 * h + 64] = total
            else:
                low[s] = total.astype(BF16)
            if f == 2:
                back[h, "q0"] = link.start(low.at[pl.ds(128, 32)], xp0.at[h], **{a: 1})
                back[h, "n0"] = link.start(low.at[pl.ds(160, 32)], xm0.at[h], **{a: -1})
            if f == 1:
                back[h, "q1"] = link.start(low.at[pl.ds(96, 32)], xp1.at[h, pl.ds(32, 32)], **{a: 1})
            if f == 3:
                back[h, "n1"] = link.start(low.at[pl.ds(192, 32)], xm1.at[h, pl.ds(0, 32)], **{a: -1})

    def outer(h):
        a = axes[h][0]
        low = (low_a, low_b)[h]
        back[h, "q0"].wait_recv()
        add_into(low.at[pl.ds(64, 32)], low[64:96], xp0[h])
        back[h, "q2"] = link.start(low.at[pl.ds(64, 32)], xp1.at[h, pl.ds(0, 32)], **{a: 1})
        back[h, "n0"].wait_recv()
        add_into(low.at[pl.ds(224, 32)], low[224:256], xm0[h])
        back[h, "n2"] = link.start(low.at[pl.ds(224, 32)], xm1.at[h, pl.ds(32, 32)], **{a: -1})

    z0p.wait_recv()
    add_into(dq(1, 0, 64), dq(1, 0, 64)[...], zp0[...])
    z2p = link.start(dq(1, 0, 64), zp1.at[pl.ds(0, 64)], dz=1)
    z0m.wait_recv()
    add_into(dq(3, 64, 64), dq(3, 64, 64)[...], zm0[...])
    z2m = link.start(dq(3, 64, 64), zm1.at[pl.ds(64, 64)], dz=-1)
    inner(0)
    inner(1)
    home[0].wait_recv()
    for copy in (z1p, z2p, z1m, z2m):
        copy.wait_recv()
    d_q = (
        dq(0)[...].astype(F32)
        + sib[PLACE[0]].astype(F32)
        + zp1[...].astype(F32)
        + zm1[...].astype(F32)
    )
    dz_ref[0:128] = norm_back(d_q, qu_ref[...], qi_ref[...])
    pair_q = link.start(dz_ref.at[pl.ds(0, 128)], dz_ref.at[pl.ds(256, 128)], dk=1)
    outer(0)
    outer(1)
    for h in (0, 1):
        for name in ("q1", "q2", "n1", "n2"):
            back[h, name].wait_recv()
        s = slice(64 * h, 64 * h + 64)
        dc_sum[s] = dc_sum[s] + xp1[h].astype(F32) + xm1[h].astype(F32)
    dz_ref[128:256] = norm_back(dc_sum[...], cu_ref[...], ci_ref[...])
    pair_c = link.start(dz_ref.at[pl.ds(128, 128)], dz_ref.at[pl.ds(384, 128)], dk=1)
    pair_q.wait_recv()
    pair_c.wait_recv()
    for move in moves:
        move.wait()
    for copy in shared:
        copy.wait_recv()
    link.drain()


N_ATTEND = 7 + 4 + 3 + 16 + 4 + 8 + 2 + 3 + 16 + 7 + 12 + 4 + 6 + 12 + 2


PARTS = ((0, 384, "zxy"), (384, 384, "xyz"), (768, 256, "yzx"))


def finish(dz_ref, half_ref, w_hbm, qg_ref, cg_ref, pg_ref, weights, partial, *rest):
    boxes, (send, recv, local) = rest[:-3], rest[-3:]
    link = Links(send, recv)
    fetch = pltpu.make_async_copy(w_hbm, weights, local)
    fetch.start()
    link.barrier([{f"d{a}": s} for a in "xyz" for s in (1, -1)])
    here = {"x": link.x, "y": link.y, "z": link.z}
    per = len(boxes) // len(PARTS)
    rows_q = pg_ref.shape[0]
    low, high = pl.ds(0, rows_q // 2), pl.ds(rows_q // 2, rows_q // 2)

    class Part:
        def __init__(self, i):
            self.at, self.n, self.order = PARTS[i]
            self.boxes = boxes[per * i : per * i + per]
            self.left = "zxy"
            self.level = 0
            self.value = None

        def chunk(self, d, rows=slice(None)):
            axis = self.order[self.level]
            index = tuple(
                (here[a] + d) % 4 if a == axis else slice(None) for a in self.left
            )
            if self.level == 0:
                return partial.at[index + (rows, pl.ds(self.at, self.n))]
            return self.value.at[index + (rows,)]

        def box(self, name):
            return self.boxes[5 * self.level + ("p0", "m0", "p1", "m1", "sum").index(name)]

        def rows_of(self, ref, rows):
            return ref.at[(slice(None),) * (len(self.left) - 1) + (rows,)]

        def open(self):
            name = "d" + self.order[self.level]
            self.c = {}
            self.c["p0"] = link.start(self.chunk(2, low), self.box("p0"), **{name: 1})
            self.c["m0"] = link.start(self.chunk(2, high), self.box("m0"), **{name: -1})
            self.c["p1"] = link.start(
                self.chunk(1, high), self.rows_of(self.box("p1"), high), **{name: 1}
            )
            self.c["m1"] = link.start(
                self.chunk(3, low), self.rows_of(self.box("m1"), low), **{name: -1}
            )

        def merge(self, dst, *terms):
            if len(dst.shape) <= 2:
                add_into(dst, *[t[...] for t in terms])
                return

            def body(i, carry):
                add_into(dst.at[i], *[t[i] for t in terms])
                return carry

            lax.fori_loop(0, dst.shape[0], body, 0)

        def relay(self):
            name = "d" + self.order[self.level]
            self.c["p0"].wait_recv()
            self.merge(self.chunk(1, low), self.chunk(1, low), self.box("p0"))
            self.c["p2"] = link.start(
                self.chunk(1, low), self.rows_of(self.box("p1"), low), **{name: 1}
            )
            self.c["m0"].wait_recv()
            self.merge(self.chunk(3, high), self.chunk(3, high), self.box("m0"))
            self.c["m2"] = link.start(
                self.chunk(3, high), self.rows_of(self.box("m1"), high), **{name: -1}
            )

        def close(self):
            for key in ("p1", "p2", "m1", "m2"):
                self.c[key].wait_recv()
            terms = (self.chunk(0), self.box("p1"), self.box("m1"))
            if self.level == 2:
                total = sum(t[...].astype(F32) for t in terms)
                pg_ref[:, self.at : self.at + self.n] = total
                return
            done = self.box("sum")
            self.merge(done, *terms)
            self.value = done
            self.left = self.left.replace(self.order[self.level], "")
            self.level += 1

    parts = [Part(i) for i in range(len(PARTS))]
    for part in (parts[2], parts[0], parts[1]):
        cols = pl.ds(part.at, part.n)

        def product(i, carry, cols=cols, n=part.n):
            rows = pl.ds(pl.multiple_of(256 * i, 256), 256)
            value = dot_tn(half_ref[:, rows], dz_ref[:, cols]).astype(BF16)
            partial[i // 2, pl.ds(2 * (i % 2), 2), :, :, cols] = value.reshape(2, 4, 32, n)
            return carry

        lax.fori_loop(0, 8, product, 0)
        part.open()

    fetch.wait()

    def features(i, carry):
        rows = pl.ds(pl.multiple_of(256 * i, 256), 256)
        value = dot_nt(dz_ref[0:256], weights[rows]).astype(BF16)
        qg_ref[:, rows] = value[0:128]
        cg_ref[:, rows] = value[128:256]
        return carry

    order = (parts[2], parts[0], parts[1])
    lax.fori_loop(0, 8, features, 0)
    for part in order:
        part.relay()
    lax.fori_loop(8, 16, features, 0)
    for part in order:
        part.close()
        part.open()
    for level in (1, 2):
        for part in order:
            part.relay()
        for part in order:
            part.close()
            if level == 1:
                part.open()
    link.drain()


def embed(features, projection):
    values = jnp.dot(features, projection, preferred_element_type=F32)
    inverse = lax.rsqrt(jnp.sum(values * values, axis=1, keepdims=True) + epsilon)
    unit_vec = values * inverse
    return (unit_vec, inverse, unit_vec.astype(BF16))


def notes_of(hard_ids, loss_weight):
    group, member = lax.axis_index("group"), lax.axis_index("member")
    z, core, x, y = group // 2, group % 2, member // 4, member % 4
    line = jnp.array(LINE, jnp.int32)
    at = 2 * ((z + line[:, 0]) % 4) + (core + line[:, 1]) % 2
    t = jnp.arange(8, dtype=jnp.int32)[:, None]
    u = jnp.arange(4, dtype=jnp.int32)[None, :]
    dx = jnp.where(t < 4, u, t - 4)
    dy = jnp.where(t < 4, t, u)
    block = ((4 * ((x + dx) % 4) + (y + dy) % 4) * 2 + t // 4).reshape(-1)
    ids = at[:, None] * 32 + block[None, :]
    wanted = jnp.any(ids[:, :, None] == hard_ids[0][None, None, :], axis=2)
    wanted = wanted | (at == group)[:, None]
    bias = jnp.where(wanted, 0.0, LOW).astype(F32)
    bias = jnp.broadcast_to(bias[:, :, None], (8, 32, 128))
    weight = jnp.broadcast_to(loss_weight[None, None, :], (8, 8, 128))
    return jnp.concatenate([bias, weight], axis=1)


def body(query_feat, code_feat, projection, hard_ids, loss_weight):
    rows, depth = query_feat.shape
    width = projection.shape[1]
    q_unit, q_inv, q_emb = embed(query_feat, projection)
    c_unit, c_inv, c_emb = embed(code_feat, projection)
    notes = notes_of(hard_ids, loss_weight)
    vmem = pl.BlockSpec(memory_space=pltpu.VMEM)
    anywhere = pl.BlockSpec(memory_space=pl.ANY)

    def vm(*shape, dtype=BF16):
        return pltpu.VMEM(shape, dtype)

    dz, half = pl.pallas_call(
        attend,
        out_shape=(
            jax.ShapeDtypeStruct((4 * rows, width), BF16),
            jax.ShapeDtypeStruct((4 * rows, depth // 2), BF16),
        ),
        in_specs=[vmem] * 7 + [anywhere] * 2,
        out_specs=(vmem, anywhere),
        scratch_shapes=[
            vm(1024, width),
            vm(2048, width),
            vm(2048, 1024, dtype=F32),
            vm(2048, 1024),
            vm(2048, width),
            vm(1024, width),
            vm(8, 40, 128, dtype=F32),
            vm(16, 128, dtype=F32),
            vm(8, 16, 128, dtype=F32),
            vm(1, 1024, dtype=F32),
            vm(1, 1024, dtype=F32),
            vm(1, 1024, dtype=F32),
            vm(1, 1024, dtype=F32),
            vm(2, 128, width),
            vm(2, 128, width),
            vm(2, 256, width),
            vm(2, 256, width),
            vm(2, 32, width),
            vm(2, 32, width),
            vm(2, 64, width),
            vm(2, 64, width),
            vm(4, 128, width),
            vm(64, width),
            vm(64, width),
            vm(128, width),
            vm(128, width),
            vm(256, width),
            vm(256, width),
            vm(128, width, dtype=F32),
            pltpu.SemaphoreType.DMA((N_ATTEND,)),
            pltpu.SemaphoreType.DMA((N_ATTEND,)),
            pltpu.SemaphoreType.DMA((8,)),
        ],
        compiler_params=pltpu.CompilerParams(
            collective_id=0, has_side_effects=True, vmem_limit_bytes=56 * 2**20
        ),
        name="attend",
    )(q_emb, c_emb, notes, q_unit, q_inv, c_unit, c_inv, query_feat, code_feat)

    boxes = []
    for _, n, _ in PARTS:
        for dims in ((4, 4), (4,), ()):
            boxes += [vm(*dims, 16, n)] * 2 + [vm(*dims, 32, n)] * 3
    return tuple(
        pl.pallas_call(
            finish,
            out_shape=(
                jax.ShapeDtypeStruct((rows, depth), BF16),
                jax.ShapeDtypeStruct((rows, depth), BF16),
                jax.ShapeDtypeStruct((depth // 128, width), F32),
            ),
            in_specs=[vmem, vmem, anywhere],
            out_specs=(vmem, vmem, vmem),
            scratch_shapes=[vm(depth, width), vm(4, 4, 4, 32, width), *boxes]
            + [
                pltpu.SemaphoreType.DMA((54,)),
                pltpu.SemaphoreType.DMA((54,)),
                pltpu.SemaphoreType.DMA,
            ],
            compiler_params=pltpu.CompilerParams(
                collective_id=1, has_side_effects=True, vmem_limit_bytes=56 * 2**20
            ),
            name="finish",
        )(dz, half, projection)
    )


def solution(mesh):
    lined = P(("group", "member"), None)
    return jax.shard_map(
        body,
        mesh=mesh,
        in_specs=(lined, lined, P(), lined, P(("group", "member"))),
        out_specs=(lined, lined, lined),
        check_vma=False,
    )
```

```python
import functools

import jax
import jax.numpy as jnp
from jax import lax
from jax.experimental import pallas as pl
from jax.experimental.pallas import tpu as pltpu
from jax.sharding import PartitionSpec as P

MESH = pl.DeviceIdType.MESH
F32 = jnp.float32
BF16 = jnp.bfloat16
inverse_temp = 120.0
epsilon = 1e-06
LOW = -1e30

PLACE = {2: 0, 1: 1, 3: 2, 0: 3}
LINE = [(dz, dk) for dz in (2, 1, 3, 0) for dk in (0, 1)]
PEERS = [p for p in LINE if p != (0, 0)]


def slot(dz, dk):
    return 2 * PLACE[dz % 4] + dk % 2


OWN = slot(0, 0)


class Links:
    def __init__(self, send, recv):
        self.send, self.recv, self.made = send, recv, []
        group, member = lax.axis_index("group"), lax.axis_index("member")
        self.z, self.core = group // 2, group % 2
        self.x, self.y = member // 4, member % 4

    def device(self, dx=0, dy=0, dz=0, dk=0):
        group = 2 * ((self.z + dz % 4) % 4) + (self.core + dk) % 2
        member = 4 * ((self.x + dx % 4) % 4) + (self.y + dy % 4) % 4
        return (group, member)

    def start(self, src, dst, **where):
        i = len(self.made)
        copy = pltpu.make_async_remote_copy(
            src_ref=src,
            dst_ref=dst,
            send_sem=self.send.at[i],
            recv_sem=self.recv.at[i],
            device_id=self.device(**where),
            device_id_type=MESH,
        )
        copy.start()
        self.made.append(copy)
        return copy

    def greet(self):
        sem = pltpu.get_barrier_semaphore()
        places = [dict(dx=1), dict(dx=-1), dict(dy=1), dict(dy=-1)]
        places += [dict(dz=dz, dk=dk) for dz, dk in PEERS]
        for where in places:
            pl.semaphore_signal(sem, inc=1, device_id=self.device(**where), device_id_type=MESH)

    def meet(self):
        pl.semaphore_wait(pltpu.get_barrier_semaphore(), 4 + len(PEERS))

    def drain(self):
        for copy in self.made:
            copy.wait_send()


def dot_nt(a, b):
    return lax.dot_general(a, b, (((1,), (1,)), ((), ())), preferred_element_type=F32)


def add_into(dst, *terms):
    total = terms[0].astype(F32)
    for term in terms[1:]:
        total = total + term.astype(F32)
    dst[...] = total.astype(dst.dtype)


def norm_back(upstream, unit, inverse):
    inner = jnp.sum(unit * upstream, axis=1, keepdims=True)
    return (inverse * (upstream - unit * inner)).astype(BF16)


PARTS = ((0, 384, "zxy"), (384, 384, "xyz"), (768, 256, "yzx"))

N_COPIES = 7 + 4 + 3 + 16 + 4 + 4 + 2 + 3 + 16 + 7 + 12 + 4 + 6 + 12 + 2 + 54


def step(
    qf_hbm, cf_hbm, w_hbm, ids_ref, weight_ref,
    qg_ref, cg_ref, pg_ref,
    outbox, weights, partial, feats, other, turned, unit, inverse, dz_ref,
    queries, codes, scores, grads, turn, dcode, dquery, notes, mine, stats, top, mass, lse, scale,
    yp0, ym0, yp1, ym1, xp0, xm0, xp1, xm1, sib, zp0, zm0, zp1, zm1, low_a, low_b, dc_sum,
    *rest,
):
    boxes, (send, recv, local) = rest[:-3], rest[-3:]
    width = weights.shape[1]
    link = Links(send, recv)
    loads = [
        pltpu.make_async_copy(f, feats.at[pl.ds(128 * i, 128)], local.at[i])
        for i, f in enumerate((qf_hbm, cf_hbm))
    ]
    fetch = [
        pltpu.make_async_copy(
            w_hbm.at[:, pl.ds(256 * n, 256)], weights.at[:, pl.ds(256 * n, 256)], local.at[2 + n]
        )
        for n in range(4)
    ]
    for load in loads + fetch:
        load.start()
    link.greet()

    row = lax.broadcasted_iota(jnp.int32, (32, 128), 0)
    first, second, half = row % 4, (row // 4) % 4, row // 16
    ax = (link.x + jnp.where(half == 0, first, second)) % 4
    ay = (link.y + jnp.where(half == 0, second, first)) % 4
    block = (4 * ax + ay) * 2 + half
    for dz, dk in LINE:
        if (dz, dk) == (0, 0):
            bias = jnp.zeros((32, 128), F32)
        else:
            base = 32 * (2 * ((link.z + dz) % 4) + (link.core + dk) % 2)
            bias = jnp.full((32, 128), LOW, F32)
            for i in range(ids_ref.shape[1]):
                bias = jnp.where(block == ids_ref[0, i] - base, 0.0, bias)
        outbox[slot(dz, dk), 0:32] = bias
        outbox[slot(dz, dk), 32:40] = jnp.broadcast_to(weight_ref[...], (8, 128))

    for load in loads:
        load.wait()
    link.meet()

    shared = []
    for zz in range(4):
        give = pl.ds(pl.multiple_of((2 * zz + 1 - link.core) * 512, 512), 512)
        shared.append(link.start(feats.at[:, give], other.at[:, pl.ds(512 * zz, 512)], dk=1))

    for n in range(4):
        fetch[n].wait()
        unit[:, 256 * n : 256 * n + 256] = jnp.dot(
            feats[...], weights[:, 256 * n : 256 * n + 256], preferred_element_type=F32
        )
    values = unit[...]
    inverse[...] = lax.rsqrt(jnp.sum(values * values, axis=1, keepdims=True) + epsilon)
    unit[...] = unit[...] * inverse[...]

    def q_rows(dz, dk, at=0, n=128):
        return queries.at[pl.ds(128 * slot(dz, dk) + at, n)]

    def code(half, first, second, at=0, n=64):
        return codes.at[pl.ds(256 * (4 * half + second) + 64 * first + at, n)]

    axes = (("dx", "dy"), ("dy", "dx"))

    codes[0:64] = unit[128:192].astype(BF16)
    codes[1024:1088] = unit[192:256].astype(BF16)
    near = {}
    for h in (0, 1):
        a = axes[h][0]
        near[h, 3] = link.start(code(h, 0, 0), code(h, 3, 0), **{a: 1})
        near[h, 1] = link.start(code(h, 0, 0), code(h, 1, 0), **{a: -1})
    queries[pl.ds(128 * OWN, 128)] = unit[0:128].astype(BF16)
    q_in = {}
    q_in[3] = link.start(q_rows(0, 0), q_rows(3, 0), dz=1)
    q_in[1] = link.start(q_rows(0, 0), q_rows(1, 0), dz=-1)
    s_in = {0: link.start(q_rows(0, 0), q_rows(0, 1), dk=1)}
    note_in = {}
    for dz, dk in PEERS:
        s, r = slot(dz, dk), slot(-dz, dk)
        note_in[r] = link.start(outbox.at[s], notes.at[r], dz=dz, dk=dk)
    notes[OWN] = outbox[OWN]

    step = {}

    def spread(h, f):
        b = axes[h][1]
        step[h, f, 3] = link.start(code(h, f, 0), code(h, f, 3), **{b: 1})
        step[h, f, 1] = link.start(code(h, f, 0), code(h, f, 1), **{b: -1})

    far = {}
    for h in (0, 1):
        spread(h, 0)
    for h in (0, 1):
        a = axes[h][0]
        near[h, 1].wait_recv()
        far[h, 0] = link.start(code(h, 1, 0, 0, 32), code(h, 2, 0, 0, 32), **{a: -1})
        spread(h, 1)
        near[h, 3].wait_recv()
        far[h, 1] = link.start(code(h, 3, 0, 32, 32), code(h, 2, 0, 32, 32), **{a: 1})
        spread(h, 3)

    top[...] = jnp.full(top.shape, LOW, F32)
    mass[...] = jnp.zeros(mass.shape, F32)

    q_in[1].wait_recv()
    q_far0 = link.start(q_rows(1, 0, 0, 64), q_rows(2, 0, 0, 64), dz=-1)
    s_in[1] = link.start(q_rows(1, 0), q_rows(1, 1), dk=1)
    q_in[3].wait_recv()
    q_far1 = link.start(q_rows(3, 0, 64, 64), q_rows(2, 0, 64, 64), dz=1)
    s_in[3] = link.start(q_rows(3, 0), q_rows(3, 1), dk=1)
    for h in (0, 1):
        far[h, 0].wait_recv()
        far[h, 1].wait_recv()
        spread(h, 2)

    last = {}

    def onward(f):
        for h in (0, 1):
            b = axes[h][1]
            step[h, f, 1].wait_recv()
            last[h, f, 0] = link.start(code(h, f, 1, 0, 32), code(h, f, 2, 0, 32), **{b: -1})
            step[h, f, 3].wait_recv()
            last[h, f, 1] = link.start(code(h, f, 3, 32, 32), code(h, f, 2, 32, 32), **{b: 1})

    def score(t):
        rows = pl.ds(256 * t, 256)

        def part(j, carry):
            lanes = pl.ds(pl.multiple_of(256 * j, 256), 256)
            s = inverse_temp * dot_nt(codes[rows], queries[pl.ds(pl.multiple_of(256 * j, 256), 256)])
            pieces = []
            for u in range(4):
                bias = jnp.concatenate(
                    [notes[2 * j, 4 * t + u : 4 * t + u + 1], notes[2 * j + 1, 4 * t + u : 4 * t + u + 1]],
                    axis=1,
                )
                pieces.append(s[64 * u : 64 * u + 64] + bias)
            s = jnp.concatenate(pieces, axis=0)
            scores[rows, lanes] = s
            before = top[:, lanes]
            after = jnp.maximum(before, jnp.max(s, axis=0, keepdims=True))
            mass[:, lanes] = mass[:, lanes] * jnp.exp(before - after) + jnp.sum(
                jnp.exp(s - after), axis=0, keepdims=True
            )
            top[:, lanes] = after
            return carry

        lax.fori_loop(0, 4, part, 0)

    onward(0)
    onward(1)
    for copy in shared:
        copy.wait_recv()
    for zz in range(4):
        keep = pl.ds(pl.multiple_of((2 * zz + link.core) * 512, 512), 512)
        rows = slice(512 * zz, 512 * zz + 512)
        turned[rows, 0:256] = feats[:, keep].T
        turned[rows, 256:512] = other[:, rows].T
    q_far0.wait_recv()
    q_far1.wait_recv()
    s_in[2] = link.start(q_rows(2, 0), q_rows(2, 1), dk=1)
    onward(3)
    for copy in note_in.values():
        copy.wait_recv()
    for dz in (0, 1, 3, 2):
        s_in[dz].wait_recv()
    score(0)
    score(4)
    onward(2)
    for t in (1, 3, 5, 7):
        score(t)
    for h in (0, 1):
        for f in range(4):
            last[h, f, 0].wait_recv()
            last[h, f, 1].wait_recv()
        score(4 * h + 2)

    for s in range(8):
        mine[s : s + 1] = top[:, 128 * s : 128 * s + 128]
        mine[8 + s : 9 + s] = mass[:, 128 * s : 128 * s + 128]
    told = []
    for dz, dk in PEERS:
        told.append(link.start(mine, stats.at[slot(-dz, dk)], dz=dz, dk=dk))
    stats[OWN] = mine[...]
    for copy in told:
        copy.wait_recv()
    for tz, tk in LINE:
        t = slot(tz, tk)
        seen = [(slot(rz, rk), slot(tz - rz, tk + rk)) for rz, rk in LINE]
        most = functools.reduce(jnp.maximum, [stats[r, i : i + 1] for r, i in seen])
        whole = sum(stats[r, 8 + i : 9 + i] * jnp.exp(stats[r, i : i + 1] - most) for r, i in seen)
        lse[:, 128 * t : 128 * t + 128] = most + jnp.log(whole)
        scale[:, 128 * t : 128 * t + 128] = inverse_temp * notes[t, 32:33]

    def backward(t):
        rows = pl.ds(256 * t, 256)

        def part(j, carry):
            lanes = pl.ds(pl.multiple_of(256 * j, 256), 256)
            grads[rows, lanes] = (
                scale[:, lanes] * jnp.exp(scores[rows, lanes] - lse[:, lanes])
            ).astype(BF16)
            return carry

        lax.fori_loop(0, 4, part, 0)
        if t % 4 == 0:
            lanes = slice(128 * OWN, 128 * OWN + 128)
            own = slice(256 * t, 256 * t + 64)
            i = lax.broadcasted_iota(jnp.int32, (64, 128), 0) + 16 * t
            j = lax.broadcasted_iota(jnp.int32, (64, 128), 1)
            hit = jnp.where(i == j, 1.0, 0.0).astype(F32)
            grads[own, lanes] = (
                scale[:, lanes] * (jnp.exp(scores[own, lanes] - lse[:, lanes]) - hit)
            ).astype(BF16)

        def product(n, carry):
            cols = pl.ds(pl.multiple_of(256 * n, 256), 256)
            dcode[rows, cols] = jnp.dot(
                grads[rows, :], queries[:, cols], preferred_element_type=F32
            ).astype(BF16)
            return carry

        lax.fori_loop(0, width // 256, product, 0)

    def tile(h, t, at, n):
        return dcode.at[pl.ds(256 * (4 * h + t) + at, n)]

    back = {}
    for h in (0, 1):
        b = axes[h][1]
        backward(4 * h + 2)
        back[h, "p0"] = link.start(tile(h, 2, 0, 128), yp0.at[h], **{b: 1})
        back[h, "m0"] = link.start(tile(h, 2, 128, 128), ym0.at[h], **{b: -1})
    for h in (0, 1):
        b = axes[h][1]
        backward(4 * h + 1)
        back[h, "p1"] = link.start(tile(h, 1, 128, 128), yp1.at[h, pl.ds(128, 128)], **{b: 1})
        backward(4 * h + 3)
        back[h, "m1"] = link.start(tile(h, 3, 0, 128), ym1.at[h, pl.ds(0, 128)], **{b: -1})
    for h in (0, 1):
        b = axes[h][1]
        back[h, "p0"].wait_recv()
        add_into(tile(h, 1, 0, 128), tile(h, 1, 0, 128)[...], yp0[h])
        back[h, "p2"] = link.start(tile(h, 1, 0, 128), yp1.at[h, pl.ds(0, 128)], **{b: 1})
        back[h, "m0"].wait_recv()
        add_into(tile(h, 3, 128, 128), tile(h, 3, 128, 128)[...], ym0[h])
        back[h, "m2"] = link.start(tile(h, 3, 128, 128), ym1.at[h, pl.ds(128, 128)], **{b: -1})
    backward(0)
    backward(4)

    home = {}
    for p, dz in enumerate((2, 1, 3, 0)):
        at = pl.ds(256 * p, 256)
        turn[...] = grads[:, 256 * p : 256 * p + 256].T

        def product(n, carry, at=at):
            cols = pl.ds(pl.multiple_of(256 * n, 256), 256)
            dquery[at, cols] = jnp.dot(
                turn[...], codes[:, cols], preferred_element_type=F32
            ).astype(BF16)
            return carry

        lax.fori_loop(0, width // 256, product, 0)
        home[dz] = link.start(dquery.at[pl.ds(256 * p + 128, 128)], sib.at[p], dk=1)

    def dq(dz, at=0, n=128):
        return dquery.at[pl.ds(128 * slot(dz, 0) + at, n)]

    for dz in (2, 1, 3):
        home[dz].wait_recv()
        add_into(dq(dz), dq(dz)[...], sib[PLACE[dz]])
        if dz == 2:
            z0p = link.start(dq(2, 0, 64), zp0, dz=1)
            z0m = link.start(dq(2, 64, 64), zm0, dz=-1)
        elif dz == 1:
            z1p = link.start(dq(1, 64, 64), zp1.at[pl.ds(64, 64)], dz=1)
        else:
            z1m = link.start(dq(3, 0, 64), zm1.at[pl.ds(0, 64)], dz=-1)

    def inner(h):
        a = axes[h][0]
        for name in ("p1", "p2", "m1", "m2"):
            back[h, name].wait_recv()
        low = (low_a, low_b)[h]
        for f in (2, 1, 3, 0):
            s = slice(64 * f, 64 * f + 64)
            total = (
                tile(h, 0, 64 * f, 64)[...].astype(F32)
                + yp1[h, s].astype(F32)
                + ym1[h, s].astype(F32)
            )
            if f == 0:
                dc_sum[64 * h : 64 * h + 64] = total
            else:
                low[s] = total.astype(BF16)
            if f == 2:
                back[h, "q0"] = link.start(low.at[pl.ds(128, 32)], xp0.at[h], **{a: 1})
                back[h, "n0"] = link.start(low.at[pl.ds(160, 32)], xm0.at[h], **{a: -1})
            if f == 1:
                back[h, "q1"] = link.start(low.at[pl.ds(96, 32)], xp1.at[h, pl.ds(32, 32)], **{a: 1})
            if f == 3:
                back[h, "n1"] = link.start(low.at[pl.ds(192, 32)], xm1.at[h, pl.ds(0, 32)], **{a: -1})

    def outer(h):
        a = axes[h][0]
        low = (low_a, low_b)[h]
        back[h, "q0"].wait_recv()
        add_into(low.at[pl.ds(64, 32)], low[64:96], xp0[h])
        back[h, "q2"] = link.start(low.at[pl.ds(64, 32)], xp1.at[h, pl.ds(0, 32)], **{a: 1})
        back[h, "n0"].wait_recv()
        add_into(low.at[pl.ds(224, 32)], low[224:256], xm0[h])
        back[h, "n2"] = link.start(low.at[pl.ds(224, 32)], xm1.at[h, pl.ds(32, 32)], **{a: -1})

    z0p.wait_recv()
    add_into(dq(1, 0, 64), dq(1, 0, 64)[...], zp0[...])
    z2p = link.start(dq(1, 0, 64), zp1.at[pl.ds(0, 64)], dz=1)
    z0m.wait_recv()
    add_into(dq(3, 64, 64), dq(3, 64, 64)[...], zm0[...])
    z2m = link.start(dq(3, 64, 64), zm1.at[pl.ds(64, 64)], dz=-1)
    inner(0)
    inner(1)
    home[0].wait_recv()
    for copy in (z1p, z2p, z1m, z2m):
        copy.wait_recv()
    d_q = (
        dq(0)[...].astype(F32)
        + sib[PLACE[0]].astype(F32)
        + zp1[...].astype(F32)
        + zm1[...].astype(F32)
    )
    dz_ref[0:128] = norm_back(d_q, unit[0:128], inverse[0:128])
    pair_q = link.start(dz_ref.at[pl.ds(0, 128)], dz_ref.at[pl.ds(256, 128)], dk=1)
    outer(0)
    outer(1)
    for h in (0, 1):
        for name in ("q1", "q2", "n1", "n2"):
            back[h, name].wait_recv()
        s = slice(64 * h, 64 * h + 64)
        dc_sum[s] = dc_sum[s] + xp1[h].astype(F32) + xm1[h].astype(F32)
    dz_ref[128:256] = norm_back(dc_sum[...], unit[128:256], inverse[128:256])
    pair_c = link.start(dz_ref.at[pl.ds(128, 128)], dz_ref.at[pl.ds(384, 128)], dk=1)
    pair_q.wait_recv()
    pair_c.wait_recv()
    here = {"x": link.x, "y": link.y, "z": link.z}
    per = len(boxes) // len(PARTS)
    rows_q = pg_ref.shape[0]
    low, high = pl.ds(0, rows_q // 2), pl.ds(rows_q // 2, rows_q // 2)

    class Part:
        def __init__(self, i):
            self.at, self.n, self.order = PARTS[i]
            self.boxes = boxes[per * i : per * i + per]
            self.left = "zxy"
            self.level = 0
            self.value = None

        def chunk(self, d, rows=slice(None)):
            axis = self.order[self.level]
            index = tuple(
                (here[a] + d) % 4 if a == axis else slice(None) for a in self.left
            )
            if self.level == 0:
                return partial.at[index + (rows, pl.ds(self.at, self.n))]
            return self.value.at[index + (rows,)]

        def box(self, name):
            return self.boxes[5 * self.level + ("p0", "m0", "p1", "m1", "sum").index(name)]

        def rows_of(self, ref, rows):
            return ref.at[(slice(None),) * (len(self.left) - 1) + (rows,)]

        def open(self):
            name = "d" + self.order[self.level]
            self.c = {}
            self.c["p0"] = link.start(self.chunk(2, low), self.box("p0"), **{name: 1})
            self.c["m0"] = link.start(self.chunk(2, high), self.box("m0"), **{name: -1})
            self.c["p1"] = link.start(
                self.chunk(1, high), self.rows_of(self.box("p1"), high), **{name: 1}
            )
            self.c["m1"] = link.start(
                self.chunk(3, low), self.rows_of(self.box("m1"), low), **{name: -1}
            )

        def merge(self, dst, *terms):
            if len(dst.shape) <= 2:
                add_into(dst, *[t[...] for t in terms])
                return

            def body(i, carry):
                add_into(dst.at[i], *[t[i] for t in terms])
                return carry

            lax.fori_loop(0, dst.shape[0], body, 0)

        def relay(self):
            name = "d" + self.order[self.level]
            self.c["p0"].wait_recv()
            self.merge(self.chunk(1, low), self.chunk(1, low), self.box("p0"))
            self.c["p2"] = link.start(
                self.chunk(1, low), self.rows_of(self.box("p1"), low), **{name: 1}
            )
            self.c["m0"].wait_recv()
            self.merge(self.chunk(3, high), self.chunk(3, high), self.box("m0"))
            self.c["m2"] = link.start(
                self.chunk(3, high), self.rows_of(self.box("m1"), high), **{name: -1}
            )

        def close(self):
            for key in ("p1", "p2", "m1", "m2"):
                self.c[key].wait_recv()
            terms = (self.chunk(0), self.box("p1"), self.box("m1"))
            if self.level == 2:
                total = sum(t[...].astype(F32) for t in terms)
                pg_ref[:, self.at : self.at + self.n] = total
                return
            done = self.box("sum")
            self.merge(done, *terms)
            self.value = done
            self.left = self.left.replace(self.order[self.level], "")
            self.level += 1

    parts = [Part(i) for i in range(len(PARTS))]
    for part in parts:
        cols = pl.ds(part.at, part.n)

        def product(i, carry, cols=cols, n=part.n):
            rows = pl.ds(pl.multiple_of(256 * i, 256), 256)
            value = jnp.dot(
                turned[rows], dz_ref[:, cols], preferred_element_type=F32
            ).astype(BF16)
            partial[i // 2, pl.ds(2 * (i % 2), 2), :, :, cols] = value.reshape(2, 4, 32, n)
            return carry

        lax.fori_loop(0, 8, product, 0)
        part.open()

    def features(i, carry):
        rows = pl.ds(pl.multiple_of(256 * i, 256), 256)
        value = dot_nt(dz_ref[0:256], weights[rows]).astype(BF16)
        qg_ref[:, rows] = value[0:128]
        cg_ref[:, rows] = value[128:256]
        return carry

    order = parts
    lax.fori_loop(0, 8, features, 0)
    for part in order:
        part.relay()
    lax.fori_loop(8, 16, features, 0)
    for part in order:
        part.close()
        part.open()
    for level in (1, 2):
        for part in order:
            part.relay()
        for part in order:
            part.close()
            if level == 1:
                part.open()
    link.drain()


def place(*refs):
    n = len(refs) // 2
    sems = refs[-1]
    copies = [pltpu.make_async_copy(refs[i], refs[n + i], sems.at[i]) for i in range(n)]
    for copy in copies:
        copy.start()
    for copy in copies:
        copy.wait()


def body(query_feat, code_feat, projection, hard_ids, loss_weight):
    rows, depth = query_feat.shape
    width = projection.shape[1]
    vmem = pl.BlockSpec(memory_space=pltpu.VMEM)
    anywhere = pl.BlockSpec(memory_space=pl.ANY)

    def vm(*shape, dtype=BF16):
        return pltpu.VMEM(shape, dtype)

    boxes = []
    for _, n, _ in PARTS:
        for dims in ((4, 4), (4,), ()):
            boxes += [vm(*dims, 16, n)] * 2 + [vm(*dims, 32, n)] * 3
    outs = (
        jax.ShapeDtypeStruct((rows, depth), BF16),
        jax.ShapeDtypeStruct((rows, depth), BF16),
        jax.ShapeDtypeStruct((depth // 128, width), F32),
    )
    made = pl.pallas_call(
        step,
        out_shape=outs,
        in_specs=[anywhere] * 3 + [pl.BlockSpec(memory_space=pltpu.SMEM), vmem],
        out_specs=(vmem, vmem, vmem),
        scratch_shapes=[
            vm(8, 40, 128, dtype=F32),
            vm(depth, width),
            vm(4, 4, 4, 32, width),
            vm(256, depth),
            vm(256, depth // 2),
            vm(depth // 2, 512),
            vm(256, width, dtype=F32),
            vm(256, 1, dtype=F32),
            vm(512, width),
            vm(1024, width),
            vm(2048, width),
            vm(2048, 1024, dtype=F32),
            vm(2048, 1024),
            vm(256, 2048),
            vm(2048, width),
            vm(1024, width),
            vm(8, 40, 128, dtype=F32),
            vm(16, 128, dtype=F32),
            vm(8, 16, 128, dtype=F32),
            vm(1, 1024, dtype=F32),
            vm(1, 1024, dtype=F32),
            vm(1, 1024, dtype=F32),
            vm(1, 1024, dtype=F32),
            vm(2, 128, width),
            vm(2, 128, width),
            vm(2, 256, width),
            vm(2, 256, width),
            vm(2, 32, width),
            vm(2, 32, width),
            vm(2, 64, width),
            vm(2, 64, width),
            vm(4, 128, width),
            vm(64, width),
            vm(64, width),
            vm(128, width),
            vm(128, width),
            vm(256, width),
            vm(256, width),
            vm(128, width, dtype=F32),
            *boxes,
            pltpu.SemaphoreType.DMA((N_COPIES,)),
            pltpu.SemaphoreType.DMA((N_COPIES,)),
            pltpu.SemaphoreType.DMA((6,)),
        ],
        compiler_params=pltpu.CompilerParams(
            collective_id=0, has_side_effects=True, vmem_limit_bytes=60 * 2**20
        ),
        name="step",
    )(query_feat, code_feat, projection, hard_ids, loss_weight[None])
    return tuple(
        pl.pallas_call(
            place,
            out_shape=outs,
            in_specs=[vmem] * 3,
            out_specs=(anywhere,) * 3,
            scratch_shapes=[pltpu.SemaphoreType.DMA((3,))],
            name="place",
        )(*made)
    )


def solution(mesh):
    lined = P(("group", "member"), None)
    return jax.shard_map(
        body,
        mesh=mesh,
        in_specs=(lined, lined, P(), lined, P(("group", "member"))),
        out_specs=(lined, lined, lined),
        check_vma=False,
    )
```

```python
import functools

import jax
import jax.numpy as jnp
from jax import lax
from jax.experimental import pallas as pl
from jax.experimental.pallas import tpu as pltpu
from jax.sharding import PartitionSpec as P

MESH = pl.DeviceIdType.MESH
F32 = jnp.float32
BF16 = jnp.bfloat16
inverse_temp = 120.0
epsilon = 1e-06
LOW = -1e30

PLACE = {2: 0, 1: 1, 3: 2, 0: 3}
LINE = [(dz, dk) for dz in (2, 1, 3, 0) for dk in (0, 1)]
PEERS = [p for p in LINE if p != (0, 0)]


def slot(dz, dk):
    return 2 * PLACE[dz % 4] + dk % 2


OWN = slot(0, 0)


class Links:
    def __init__(self, send, recv):
        self.send, self.recv, self.made = send, recv, []
        group, member = lax.axis_index("group"), lax.axis_index("member")
        self.z, self.core = group // 2, group % 2
        self.x, self.y = member // 4, member % 4

    def device(self, dx=0, dy=0, dz=0, dk=0):
        group = 2 * ((self.z + dz % 4) % 4) + (self.core + dk) % 2
        member = 4 * ((self.x + dx % 4) % 4) + (self.y + dy % 4) % 4
        return (group, member)

    def start(self, src, dst, **where):
        i = len(self.made)
        copy = pltpu.make_async_remote_copy(
            src_ref=src,
            dst_ref=dst,
            send_sem=self.send.at[i],
            recv_sem=self.recv.at[i],
            device_id=self.device(**where),
            device_id_type=MESH,
        )
        copy.start()
        self.made.append(copy)
        return copy

    def greet(self):
        sem = pltpu.get_barrier_semaphore()
        places = [dict(dx=1), dict(dx=-1), dict(dy=1), dict(dy=-1)]
        places += [dict(dz=dz, dk=dk) for dz, dk in PEERS]
        for where in places:
            pl.semaphore_signal(sem, inc=1, device_id=self.device(**where), device_id_type=MESH)

    def meet(self):
        pl.semaphore_wait(pltpu.get_barrier_semaphore(), 4 + len(PEERS))

    def drain(self):
        for copy in self.made:
            copy.wait_send()


def dot_nt(a, b):
    return lax.dot_general(a, b, (((1,), (1,)), ((), ())), preferred_element_type=F32)


def add_into(dst, *terms):
    total = terms[0].astype(F32)
    for term in terms[1:]:
        total = total + term.astype(F32)
    dst[...] = total.astype(dst.dtype)


def norm_back(upstream, unit, inverse):
    inner = jnp.sum(unit * upstream, axis=1, keepdims=True)
    return (inverse * (upstream - unit * inner)).astype(BF16)


PARTS = ((0, 384, "zxy"), (384, 384, "xyz"), (768, 256, "yzx"))

N_COPIES = 7 + 4 + 3 + 16 + 4 + 4 + 2 + 3 + 16 + 7 + 12 + 4 + 6 + 12 + 2 + 36


def step(
    qf_hbm, cf_hbm, w_hbm, ids_ref, weight_ref,
    qg_hbm, cg_hbm, pg_ref,
    fgrads, outbox, bias_ref, weights, partial, feats, other, turned, unit, inverse, dz_ref,
    queries, codes, scores, grads, turn, dcode, dquery, notes, mine, stats, top, mass, shift, scale,
    yp0, ym0, yp1, ym1, xp0, xm0, xp1, xm1, sib, zp0, zm0, zp1, zm1, low_a, low_b, dc_sum,
    *rest,
):
    boxes, (send, recv, local) = rest[:-3], rest[-3:]
    width = weights.shape[1]
    link = Links(send, recv)
    loads = [
        pltpu.make_async_copy(f, feats.at[pl.ds(128 * i, 128)], local.at[i])
        for i, f in enumerate((qf_hbm, cf_hbm))
    ]
    fetch = [
        pltpu.make_async_copy(
            w_hbm.at[:, pl.ds(512 * n, 512)], weights.at[:, pl.ds(512 * n, 512)], local.at[2 + n]
        )
        for n in range(2)
    ]
    for load in loads + fetch:
        load.start()
    link.greet()

    row = lax.broadcasted_iota(jnp.int32, (32, 128), 0)
    first, second, half = row % 4, (row // 4) % 4, row // 16
    ax = (link.x + jnp.where(half == 0, first, second)) % 4
    ay = (link.y + jnp.where(half == 0, second, first)) % 4
    block = (4 * ax + ay) * 2 + half
    for dz, dk in LINE:
        if (dz, dk) == (0, 0):
            bias = jnp.zeros((32, 128), F32)
        else:
            base = 32 * (2 * ((link.z + dz) % 4) + (link.core + dk) % 2)
            bias = jnp.full((32, 128), LOW, F32)
            for i in range(ids_ref.shape[1]):
                bias = jnp.where(block == ids_ref[0, i] - base, 0.0, bias)
        outbox[slot(dz, dk), 0:32] = bias
        outbox[slot(dz, dk), 32:40] = jnp.broadcast_to(weight_ref[...], (8, 128))

    def embed(rows):
        for n in range(2):
            cols = slice(512 * n, 512 * n + 512)
            unit[rows, cols] = jnp.dot(
                feats[rows], weights[:, cols], preferred_element_type=F32
            )
        values = unit[rows]
        inverse[rows] = lax.rsqrt(jnp.sum(values * values, axis=1, keepdims=True) + epsilon)
        unit[rows] = unit[rows] * inverse[rows]

    for load in loads + fetch:
        load.wait()
    embed(slice(128, 256))
    link.meet()

    def q_rows(dz, dk, at=0, n=128):
        return queries.at[pl.ds(128 * slot(dz, dk) + at, n)]

    def code(half, first, second, at=0, n=64):
        return codes.at[16 * half + 4 * second + first, pl.ds(at, n)]

    axes = (("dx", "dy"), ("dy", "dx"))

    codes[0] = unit[128:192].astype(BF16)
    codes[16] = unit[192:256].astype(BF16)
    near = {}
    for h in (0, 1):
        a = axes[h][0]
        near[h, 3] = link.start(code(h, 0, 0), code(h, 3, 0), **{a: 1})
        near[h, 1] = link.start(code(h, 0, 0), code(h, 1, 0), **{a: -1})
    step = {}

    def spread(h, f):
        b = axes[h][1]
        step[h, f, 3] = link.start(code(h, f, 0), code(h, f, 3), **{b: 1})
        step[h, f, 1] = link.start(code(h, f, 0), code(h, f, 1), **{b: -1})

    for h in (0, 1):
        spread(h, 0)
    embed(slice(0, 128))
    queries[pl.ds(128 * OWN, 128)] = unit[0:128].astype(BF16)
    q_in = {}
    q_in[3] = link.start(q_rows(0, 0), q_rows(3, 0), dz=1)
    q_in[1] = link.start(q_rows(0, 0), q_rows(1, 0), dz=-1)
    s_in = {0: link.start(q_rows(0, 0), q_rows(0, 1), dk=1)}
    note_in = {}
    for dz, dk in PEERS:
        s, r = slot(dz, dk), slot(-dz, dk)
        note_in[r] = link.start(outbox.at[s], notes.at[r], dz=dz, dk=dk)
    notes[OWN] = outbox[OWN]

    shared = []
    for zz in range(4):
        give = pl.ds(pl.multiple_of((2 * zz + 1 - link.core) * 512, 512), 512)
        shared.append(link.start(feats.at[:, give], other.at[:, pl.ds(512 * zz, 512)], dk=1))

    far = {}
    for h in (0, 1):
        a = axes[h][0]
        near[h, 1].wait_recv()
        far[h, 0] = link.start(code(h, 1, 0, 0, 32), code(h, 2, 0, 0, 32), **{a: -1})
        spread(h, 1)
        near[h, 3].wait_recv()
        far[h, 1] = link.start(code(h, 3, 0, 32, 32), code(h, 2, 0, 32, 32), **{a: 1})
        spread(h, 3)

    top[...] = jnp.full(top.shape, LOW, F32)
    mass[...] = jnp.zeros(mass.shape, F32)

    q_in[1].wait_recv()
    q_far0 = link.start(q_rows(1, 0, 0, 64), q_rows(2, 0, 0, 64), dz=-1)
    s_in[1] = link.start(q_rows(1, 0), q_rows(1, 1), dk=1)
    q_in[3].wait_recv()
    q_far1 = link.start(q_rows(3, 0, 64, 64), q_rows(2, 0, 64, 64), dz=1)
    s_in[3] = link.start(q_rows(3, 0), q_rows(3, 1), dk=1)
    for h in (0, 1):
        far[h, 0].wait_recv()
        far[h, 1].wait_recv()
        spread(h, 2)

    last = {}

    def onward(f):
        for h in (0, 1):
            b = axes[h][1]
            step[h, f, 1].wait_recv()
            last[h, f, 0] = link.start(code(h, f, 1, 0, 32), code(h, f, 2, 0, 32), **{b: -1})
            step[h, f, 3].wait_recv()
            last[h, f, 1] = link.start(code(h, f, 3, 32, 32), code(h, f, 2, 32, 32), **{b: 1})

    def score(h, f):
        ids = [16 * h + 4 * s + f for s in range(4)]
        lhs = jnp.concatenate([codes[i] for i in ids], axis=0)
        s = inverse_temp * dot_nt(lhs, queries[...])
        for u, i in enumerate(ids):
            scores[i] = s[64 * u : 64 * u + 64] + bias_ref[i : i + 1]

        def part(j, carry):
            lanes = pl.ds(pl.multiple_of(256 * j, 256), 256)
            s = jnp.concatenate([scores[i, :, lanes] for i in ids], axis=0)
            before = top[:, lanes]
            after = jnp.maximum(before, jnp.max(s, axis=0, keepdims=True))
            mass[:, lanes] = mass[:, lanes] * jnp.exp(before - after) + jnp.sum(
                jnp.exp(s - after), axis=0, keepdims=True
            )
            top[:, lanes] = after
            return carry

        lax.fori_loop(0, 4, part, 0)

    onward(0)
    onward(1)
    for copy in shared:
        copy.wait_recv()
    for zz in range(4):
        keep = pl.ds(pl.multiple_of((2 * zz + link.core) * 512, 512), 512)
        rows = slice(512 * zz, 512 * zz + 512)
        turned[rows, 0:256] = feats[:, keep].T
        turned[rows, 256:512] = other[:, rows].T
    q_far0.wait_recv()
    q_far1.wait_recv()
    s_in[2] = link.start(q_rows(2, 0), q_rows(2, 1), dk=1)
    onward(3)
    for copy in note_in.values():
        copy.wait_recv()
    for s in range(8):
        bias_ref[:, 128 * s : 128 * s + 128] = notes[s, 0:32]
    for dz in (0, 1, 3, 2):
        s_in[dz].wait_recv()
    for f in (0, 1, 3, 2):
        if f == 1:
            onward(2)
        for h in (0, 1):
            last[h, f, 0].wait_recv()
            last[h, f, 1].wait_recv()
            score(h, f)

    for s in range(8):
        mine[s : s + 1] = top[:, 128 * s : 128 * s + 128]
        mine[8 + s : 9 + s] = mass[:, 128 * s : 128 * s + 128]
    told = []
    for dz, dk in PEERS:
        told.append(link.start(mine, stats.at[slot(-dz, dk)], dz=dz, dk=dk))
    stats[OWN] = mine[...]
    for copy in told:
        copy.wait_recv()
    for tz, tk in LINE:
        t = slot(tz, tk)
        seen = [(slot(rz, rk), slot(tz - rz, tk + rk)) for rz, rk in LINE]
        most = functools.reduce(jnp.maximum, [stats[r, i : i + 1] for r, i in seen])
        whole = sum(stats[r, 8 + i : 9 + i] * jnp.exp(stats[r, i : i + 1] - most) for r, i in seen)
        factor = inverse_temp * notes[t, 32:33]
        scale[:, 128 * t : 128 * t + 128] = factor
        shift[:, 128 * t : 128 * t + 128] = most + jnp.log(whole) - jnp.log(factor)

    def gradient(t):
        rows = pl.ds(256 * t, 256)

        def part(j, carry):
            lanes = pl.ds(pl.multiple_of(256 * j, 256), 256)
            s = scores[4 * t : 4 * t + 4, :, lanes].reshape(256, 256)
            grads[rows, lanes] = jnp.exp(s - shift[:, lanes]).astype(BF16)
            return carry

        lax.fori_loop(0, 4, part, 0)
        if t % 4 == 0:
            lanes = slice(128 * OWN, 128 * OWN + 128)
            own = slice(256 * t, 256 * t + 64)
            i = lax.broadcasted_iota(jnp.int32, (64, 128), 0) + 16 * t
            j = lax.broadcasted_iota(jnp.int32, (64, 128), 1)
            hit = jnp.where(i == j, scale[:, lanes], 0.0)
            grads[own, lanes] = (
                jnp.exp(scores[4 * t, :, lanes] - shift[:, lanes]) - hit
            ).astype(BF16)

    def to_codes(t):
        rows = pl.ds(256 * t, 256)
        dcode[rows] = jnp.dot(
            grads[rows], queries[...], preferred_element_type=F32
        ).astype(BF16)

    def backward(t):
        gradient(t)
        to_codes(t)

    def tile(h, t, at, n):
        return dcode.at[pl.ds(256 * (4 * h + t) + at, n)]

    back = {}
    for h in (0, 1):
        b = axes[h][1]
        backward(4 * h + 2)
        back[h, "p0"] = link.start(tile(h, 2, 0, 128), yp0.at[h], **{b: 1})
        back[h, "m0"] = link.start(tile(h, 2, 128, 128), ym0.at[h], **{b: -1})
    for h in (0, 1):
        b = axes[h][1]
        backward(4 * h + 1)
        back[h, "p1"] = link.start(tile(h, 1, 128, 128), yp1.at[h, pl.ds(128, 128)], **{b: 1})
        backward(4 * h + 3)
        back[h, "m1"] = link.start(tile(h, 3, 0, 128), ym1.at[h, pl.ds(0, 128)], **{b: -1})
    def relay(h):
        b = axes[h][1]
        back[h, "p0"].wait_recv()
        add_into(tile(h, 1, 0, 128), tile(h, 1, 0, 128)[...], yp0[h])
        back[h, "p2"] = link.start(tile(h, 1, 0, 128), yp1.at[h, pl.ds(0, 128)], **{b: 1})
        back[h, "m0"].wait_recv()
        add_into(tile(h, 3, 128, 128), tile(h, 3, 128, 128)[...], ym0[h])
        back[h, "m2"] = link.start(tile(h, 3, 128, 128), ym1.at[h, pl.ds(128, 128)], **{b: -1})

    gradient(0)
    gradient(4)
    home = {}

    def to_queries(dz):
        p = PLACE[dz]
        turn[...] = grads[:, 256 * p : 256 * p + 256].T
        dquery[256 * p : 256 * p + 256] = jnp.dot(
            turn[...], codes[...].reshape(2048, width), preferred_element_type=F32
        ).astype(BF16)
        home[dz] = link.start(dquery.at[pl.ds(256 * p + 128, 128)], sib.at[p], dk=1)

    def dq(dz, at=0, n=128):
        return dquery.at[pl.ds(128 * slot(dz, 0) + at, n)]

    def add_sibling(dz):
        home[dz].wait_recv()
        add_into(dq(dz), dq(dz)[...], sib[PLACE[dz]])

    to_queries(2)
    to_queries(1)
    to_queries(3)
    add_sibling(2)
    z0p = link.start(dq(2, 0, 64), zp0, dz=1)
    z0m = link.start(dq(2, 64, 64), zm0, dz=-1)
    add_sibling(1)
    z1p = link.start(dq(1, 64, 64), zp1.at[pl.ds(64, 64)], dz=1)
    relay(0)
    relay(1)
    add_sibling(3)
    z1m = link.start(dq(3, 0, 64), zm1.at[pl.ds(0, 64)], dz=-1)
    to_queries(0)
    to_codes(0)
    to_codes(4)

    def inner(h):
        a = axes[h][0]
        for name in ("p1", "p2", "m1", "m2"):
            back[h, name].wait_recv()
        low = (low_a, low_b)[h]
        for f in (2, 1, 3, 0):
            s = slice(64 * f, 64 * f + 64)
            total = (
                tile(h, 0, 64 * f, 64)[...].astype(F32)
                + yp1[h, s].astype(F32)
                + ym1[h, s].astype(F32)
            )
            if f == 0:
                dc_sum[64 * h : 64 * h + 64] = total
            else:
                low[s] = total.astype(BF16)
            if f == 2:
                back[h, "q0"] = link.start(low.at[pl.ds(128, 32)], xp0.at[h], **{a: 1})
                back[h, "n0"] = link.start(low.at[pl.ds(160, 32)], xm0.at[h], **{a: -1})
            if f == 1:
                back[h, "q1"] = link.start(low.at[pl.ds(96, 32)], xp1.at[h, pl.ds(32, 32)], **{a: 1})
            if f == 3:
                back[h, "n1"] = link.start(low.at[pl.ds(192, 32)], xm1.at[h, pl.ds(0, 32)], **{a: -1})

    def outer(h):
        a = axes[h][0]
        low = (low_a, low_b)[h]
        back[h, "q0"].wait_recv()
        add_into(low.at[pl.ds(64, 32)], low[64:96], xp0[h])
        back[h, "q2"] = link.start(low.at[pl.ds(64, 32)], xp1.at[h, pl.ds(0, 32)], **{a: 1})
        back[h, "n0"].wait_recv()
        add_into(low.at[pl.ds(224, 32)], low[224:256], xm0[h])
        back[h, "n2"] = link.start(low.at[pl.ds(224, 32)], xm1.at[h, pl.ds(32, 32)], **{a: -1})

    z0p.wait_recv()
    add_into(dq(1, 0, 64), dq(1, 0, 64)[...], zp0[...])
    z2p = link.start(dq(1, 0, 64), zp1.at[pl.ds(0, 64)], dz=1)
    z0m.wait_recv()
    add_into(dq(3, 64, 64), dq(3, 64, 64)[...], zm0[...])
    z2m = link.start(dq(3, 64, 64), zm1.at[pl.ds(64, 64)], dz=-1)
    inner(0)
    inner(1)
    home[0].wait_recv()
    for copy in (z1p, z2p, z1m, z2m):
        copy.wait_recv()
    d_q = (
        dq(0)[...].astype(F32)
        + sib[PLACE[0]].astype(F32)
        + zp1[...].astype(F32)
        + zm1[...].astype(F32)
    )
    dz_ref[0:128] = norm_back(d_q, unit[0:128], inverse[0:128])
    pair_q = link.start(dz_ref.at[pl.ds(0, 128)], dz_ref.at[pl.ds(256, 128)], dk=1)
    outer(0)
    outer(1)
    for h in (0, 1):
        for name in ("q1", "q2", "n1", "n2"):
            back[h, name].wait_recv()
        s = slice(64 * h, 64 * h + 64)
        dc_sum[s] = dc_sum[s] + xp1[h].astype(F32) + xm1[h].astype(F32)
    dz_ref[128:256] = norm_back(dc_sum[...], unit[128:256], inverse[128:256])
    pair_c = link.start(dz_ref.at[pl.ds(128, 128)], dz_ref.at[pl.ds(384, 128)], dk=1)
    pair_q.wait_recv()
    pair_c.wait_recv()
    here = {"x": link.x, "y": link.y, "z": link.z}
    per = len(boxes) // len(PARTS)
    rows_q = pg_ref.shape[0]
    low, high = pl.ds(0, rows_q // 2), pl.ds(rows_q // 2, rows_q // 2)

    class Part:
        def __init__(self, i):
            self.at, self.n, self.order = PARTS[i]
            self.boxes = boxes[per * i : per * i + per]
            self.left = "zxy"
            self.level = 0
            self.value = None

        def chunk(self, d, rows=slice(None)):
            axis = self.order[self.level]
            index = tuple(
                (here[a] + d) % 4 if a == axis else slice(None) for a in self.left
            )
            if self.level == 0:
                return partial.at[index + (rows, pl.ds(self.at, self.n))]
            return self.value.at[index + (rows,)]

        def box(self, name):
            if self.level == 0:
                return self.boxes[("p0", "m0", "p1", "m1", "sum").index(name)]
            return self.boxes[1 + 4 * self.level + ("p1", "m1", "far", "sum").index(name)]

        def rows_of(self, ref, rows):
            return ref.at[(slice(None),) * (len(self.left) - 1) + (rows,)]

        def open(self, which=(2, 1, 3)):
            name = "d" + self.order[self.level]
            if 2 in which:
                self.c = {}
            if self.level:
                for d, key in ((2, "far"), (1, "p1"), (3, "m1")):
                    self.c[key] = link.start(self.chunk(d), self.box(key), **{name: d})
                return
            if 2 in which:
                self.c["p0"] = link.start(self.chunk(2, low), self.box("p0"), **{name: 1})
                self.c["m0"] = link.start(self.chunk(2, high), self.box("m0"), **{name: -1})
            if 1 in which:
                self.c["p1"] = link.start(
                    self.chunk(1, high), self.rows_of(self.box("p1"), high), **{name: 1}
                )
            if 3 in which:
                self.c["m1"] = link.start(
                    self.chunk(3, low), self.rows_of(self.box("m1"), low), **{name: -1}
                )

        def merge(self, dst, *terms):
            if len(dst.shape) <= 2:
                add_into(dst, *[t[...] for t in terms])
                return

            def body(i, carry):
                add_into(dst.at[i], *[t[i] for t in terms])
                return carry

            lax.fori_loop(0, dst.shape[0], body, 0)

        def relay(self):
            name = "d" + self.order[self.level]
            self.c["p0"].wait_recv()
            self.merge(self.chunk(1, low), self.chunk(1, low), self.box("p0"))
            self.c["p2"] = link.start(
                self.chunk(1, low), self.rows_of(self.box("p1"), low), **{name: 1}
            )
            self.c["m0"].wait_recv()
            self.merge(self.chunk(3, high), self.chunk(3, high), self.box("m0"))
            self.c["m2"] = link.start(
                self.chunk(3, high), self.rows_of(self.box("m1"), high), **{name: -1}
            )

        def close(self):
            for key, copy in self.c.items():
                if key not in ("p0", "m0"):
                    copy.wait_recv()
            terms = [self.chunk(0), self.box("p1"), self.box("m1")]
            if self.level:
                terms.append(self.box("far"))
            if self.level == 2:
                total = sum(t[...].astype(F32) for t in terms)
                pg_ref[:, self.at : self.at + self.n] = total
                return
            done = self.box("sum")
            self.merge(done, *terms)
            self.value = done
            self.left = self.left.replace(self.order[self.level], "")
            self.level += 1

    parts = [Part(i) for i in range(len(PARTS))]
    first = parts[0]
    cols = pl.ds(first.at, first.n)
    for d in (2, 1, 3, 0):
        at = (link.z + d) % 4
        rows = pl.ds(pl.multiple_of(512 * at, 512), 512)
        value = jnp.dot(turned[rows], dz_ref[:, cols], preferred_element_type=F32)
        partial[at, :, :, :, cols] = value.astype(BF16).reshape(4, 4, 32, first.n)
        if d:
            first.open((d,))
    for part in parts[1:]:
        cols = pl.ds(part.at, part.n)
        value = jnp.dot(turned[...], dz_ref[:, cols], preferred_element_type=F32)
        partial[:, :, :, :, cols] = value.astype(BF16).reshape(4, 4, 4, 32, part.n)
        part.open()

    puts = []

    def features(i):
        rows = slice(1024 * i, 1024 * i + 1024)
        fgrads[:, rows] = dot_nt(dz_ref[0:256], weights[rows]).astype(BF16)
        for n, hbm in enumerate((qg_hbm, cg_hbm)):
            put = pltpu.make_async_copy(
                fgrads.at[pl.ds(128 * n, 128), pl.ds(1024 * i, 1024)],
                hbm.at[:, pl.ds(1024 * i, 1024)],
                local.at[4 + 2 * i + n],
            )
            put.start()
            puts.append(put)

    features(0)
    features(1)
    parts[0].relay()
    features(2)
    parts[1].relay()
    parts[2].relay()
    features(3)
    for level in (0, 1, 2):
        for part in parts:
            part.close()
            if level < 2:
                part.open()
    for put in puts:
        put.wait()
    link.drain()


def place(*refs):
    n = len(refs) // 2
    sems = refs[-1]
    copies = [pltpu.make_async_copy(refs[i], refs[n + i], sems.at[i]) for i in range(n)]
    for copy in copies:
        copy.start()
    for copy in copies:
        copy.wait()


def body(query_feat, code_feat, projection, hard_ids, loss_weight):
    rows, depth = query_feat.shape
    width = projection.shape[1]
    vmem = pl.BlockSpec(memory_space=pltpu.VMEM)
    anywhere = pl.BlockSpec(memory_space=pl.ANY)

    def vm(*shape, dtype=BF16):
        return pltpu.VMEM(shape, dtype)

    boxes = []
    for _, n, _ in PARTS:
        boxes += [vm(4, 4, 16, n)] * 2 + [vm(4, 4, 32, n)] * 3
        boxes += [vm(4, 32, n)] * 4 + [vm(32, n)] * 4
    outs = (
        jax.ShapeDtypeStruct((rows, depth), BF16),
        jax.ShapeDtypeStruct((rows, depth), BF16),
        jax.ShapeDtypeStruct((depth // 128, width), F32),
    )
    made = pl.pallas_call(
        step,
        out_shape=outs,
        in_specs=[anywhere] * 3 + [pl.BlockSpec(memory_space=pltpu.SMEM), vmem],
        out_specs=(anywhere, anywhere, vmem),
        scratch_shapes=[
            vm(256, depth),
            vm(8, 40, 128, dtype=F32),
            vm(32, 1024, dtype=F32),
            vm(depth, width),
            vm(4, 4, 4, 32, width),
            vm(256, depth),
            vm(256, depth // 2),
            vm(depth // 2, 512),
            vm(256, width, dtype=F32),
            vm(256, 1, dtype=F32),
            vm(512, width),
            vm(1024, width),
            vm(32, 64, width),
            vm(32, 64, 1024, dtype=F32),
            vm(2048, 1024),
            vm(256, 2048),
            vm(2048, width),
            vm(1024, width),
            vm(8, 40, 128, dtype=F32),
            vm(16, 128, dtype=F32),
            vm(8, 16, 128, dtype=F32),
            vm(1, 1024, dtype=F32),
            vm(1, 1024, dtype=F32),
            vm(1, 1024, dtype=F32),
            vm(1, 1024, dtype=F32),
            vm(2, 128, width),
            vm(2, 128, width),
            vm(2, 256, width),
            vm(2, 256, width),
            vm(2, 32, width),
            vm(2, 32, width),
            vm(2, 64, width),
            vm(2, 64, width),
            vm(4, 128, width),
            vm(64, width),
            vm(64, width),
            vm(128, width),
            vm(128, width),
            vm(256, width),
            vm(256, width),
            vm(128, width, dtype=F32),
            *boxes,
            pltpu.SemaphoreType.DMA((N_COPIES,)),
            pltpu.SemaphoreType.DMA((N_COPIES,)),
            pltpu.SemaphoreType.DMA((12,)),
        ],
        compiler_params=pltpu.CompilerParams(
            collective_id=0, has_side_effects=True, vmem_limit_bytes=60 * 2**20
        ),
        name="step",
    )(query_feat, code_feat, projection, hard_ids, loss_weight[None])
    return tuple(
        pl.pallas_call(
            place,
            out_shape=outs,
            in_specs=[vmem] * 3,
            out_specs=(anywhere,) * 3,
            scratch_shapes=[pltpu.SemaphoreType.DMA((3,))],
            name="place",
        )(*made)
    )


def solution(mesh):
    lined = P(("group", "member"), None)
    return jax.shard_map(
        body,
        mesh=mesh,
        in_specs=(lined, lined, P(), lined, P(("group", "member"))),
        out_specs=(lined, lined, lined),
        check_vma=False,
    )
```

```python
import functools

import jax
import jax.numpy as jnp
from jax import lax
from jax.experimental import pallas as pl
from jax.experimental.pallas import tpu as pltpu
from jax.sharding import PartitionSpec as P

MESH = pl.DeviceIdType.MESH
F32 = jnp.float32
BF16 = jnp.bfloat16
inverse_temp = 120.0
epsilon = 1e-06
LOW = -1e30

PLACE = {2: 0, 1: 1, 3: 2, 0: 3}
LINE = [(dz, dk) for dz in (2, 1, 3, 0) for dk in (0, 1)]
PEERS = [p for p in LINE if p != (0, 0)]


def slot(dz, dk):
    return 2 * PLACE[dz % 4] + dk % 2


OWN = slot(0, 0)


class Links:
    def __init__(self, send, recv):
        self.send, self.recv, self.made = send, recv, []
        group, member = lax.axis_index("group"), lax.axis_index("member")
        self.z, self.core = group // 2, group % 2
        self.x, self.y = member // 4, member % 4

    def device(self, dx=0, dy=0, dz=0, dk=0):
        group = 2 * ((self.z + dz % 4) % 4) + (self.core + dk) % 2
        member = 4 * ((self.x + dx % 4) % 4) + (self.y + dy % 4) % 4
        return (group, member)

    def start(self, src, dst, **where):
        i = len(self.made)
        copy = pltpu.make_async_remote_copy(
            src_ref=src,
            dst_ref=dst,
            send_sem=self.send.at[i],
            recv_sem=self.recv.at[i],
            device_id=self.device(**where),
            device_id_type=MESH,
        )
        copy.start()
        self.made.append(copy)
        return copy

    def greet(self):
        sem = pltpu.get_barrier_semaphore()
        places = [dict(dx=1), dict(dx=-1), dict(dy=1), dict(dy=-1)]
        places += [dict(dz=dz, dk=dk) for dz, dk in PEERS]
        for where in places:
            pl.semaphore_signal(sem, inc=1, device_id=self.device(**where), device_id_type=MESH)

    def meet(self):
        pl.semaphore_wait(pltpu.get_barrier_semaphore(), 4 + len(PEERS))

    def drain(self):
        for copy in self.made:
            copy.wait_send()


def dot_nt(a, b):
    return lax.dot_general(a, b, (((1,), (1,)), ((), ())), preferred_element_type=F32)


def add_into(dst, *terms):
    total = terms[0].astype(F32)
    for term in terms[1:]:
        total = total + term.astype(F32)
    dst[...] = total.astype(dst.dtype)


def norm_back(upstream, unit, inverse):
    inner = jnp.sum(unit * upstream, axis=1, keepdims=True)
    return (inverse * (upstream - unit * inner)).astype(BF16)


PARTS = (
    (0, 256, "zxy"),
    (256, 128, "zxy"),
    (384, 256, "xyz"),
    (640, 128, "xyz"),
    (768, 128, "yzx"),
    (896, 128, "yzx"),
)

N_COPIES = 7 + 4 + 3 + 16 + 4 + 4 + 2 + 3 + 16 + 7 + 12 + 4 + 6 + 12 + 2 + 4 + 72


def step(
    qf_hbm, cf_hbm, w_hbm, ids_ref, weight_ref,
    qg_hbm, cg_hbm, pg_ref,
    fgrads, outbox, bias_ref, weights, feats, other, turned, unit, inverse, dz_ref,
    queries, codes, scores, grads, turn, dcode, dquery, notes, mine, mine_lse, stats, top, mass, shift, scale,
    yp0, ym0, yp1, ym1, xp0, xm0, xp1, xm1, sib, zp0, zm0, zp1, zm1, low_a, low_b, dc_sum,
    *rest,
):
    boxes, (send, recv, local) = rest[:-3], rest[-3:]
    partial, boxes = boxes[: len(PARTS)], boxes[len(PARTS) :]
    width = weights.shape[1]
    link = Links(send, recv)
    loads = [
        pltpu.make_async_copy(f, feats.at[pl.ds(128 * i, 128)], local.at[i])
        for i, f in enumerate((qf_hbm, cf_hbm))
    ]
    fetch = [
        pltpu.make_async_copy(
            w_hbm.at[:, pl.ds(512 * n, 512)], weights.at[:, pl.ds(512 * n, 512)], local.at[2 + n]
        )
        for n in range(2)
    ]
    for load in loads + fetch:
        load.start()
    link.greet()

    row = lax.broadcasted_iota(jnp.int32, (32, 128), 0)
    first, second, half = row % 4, (row // 4) % 4, row // 16
    ax = (link.x + jnp.where(half == 0, first, second)) % 4
    ay = (link.y + jnp.where(half == 0, second, first)) % 4
    block = (4 * ax + ay) * 2 + half
    for dz, dk in LINE:
        if (dz, dk) == (0, 0):
            bias = jnp.zeros((32, 128), F32)
        else:
            base = 32 * (2 * ((link.z + dz) % 4) + (link.core + dk) % 2)
            bias = jnp.full((32, 128), LOW, F32)
            for i in range(ids_ref.shape[1]):
                bias = jnp.where(block == ids_ref[0, i] - base, 0.0, bias)
        outbox[slot(dz, dk), 0:32] = bias
        outbox[slot(dz, dk), 32:40] = jnp.broadcast_to(weight_ref[...], (8, 128))

    def embed(rows):
        for n in range(2):
            cols = slice(512 * n, 512 * n + 512)
            unit[rows, cols] = jnp.dot(
                feats[rows], weights[:, cols], preferred_element_type=F32
            )
        values = unit[rows]
        inverse[rows] = lax.rsqrt(jnp.sum(values * values, axis=1, keepdims=True) + epsilon)
        unit[rows] = unit[rows] * inverse[rows]

    for load in loads + fetch:
        load.wait()
    embed(slice(128, 256))
    link.meet()

    def q_rows(dz, dk, at=0, n=128):
        return queries.at[pl.ds(128 * slot(dz, dk) + at, n)]

    def code(half, first, second, at=0, n=64):
        return codes.at[16 * half + 4 * second + first, pl.ds(at, n)]

    axes = (("dx", "dy"), ("dy", "dx"))

    codes[0] = unit[128:192].astype(BF16)
    codes[16] = unit[192:256].astype(BF16)
    near = {}
    for h in (0, 1):
        a = axes[h][0]
        near[h, 3] = link.start(code(h, 0, 0), code(h, 3, 0), **{a: 1})
        near[h, 1] = link.start(code(h, 0, 0), code(h, 1, 0), **{a: -1})
    step = {}

    def spread(h, f):
        b = axes[h][1]
        step[h, f, 3] = link.start(code(h, f, 0), code(h, f, 3), **{b: 1})
        step[h, f, 1] = link.start(code(h, f, 0), code(h, f, 1), **{b: -1})

    for h in (0, 1):
        spread(h, 0)
    embed(slice(0, 128))
    queries[pl.ds(128 * OWN, 128)] = unit[0:128].astype(BF16)
    q_in = {}
    q_in[3] = link.start(q_rows(0, 0), q_rows(3, 0), dz=1)
    q_in[1] = link.start(q_rows(0, 0), q_rows(1, 0), dz=-1)
    s_in = {0: link.start(q_rows(0, 0), q_rows(0, 1), dk=1)}
    note_in = {}
    for dz, dk in PEERS:
        s, r = slot(dz, dk), slot(-dz, dk)
        note_in[r] = link.start(outbox.at[s], notes.at[r], dz=dz, dk=dk)
    notes[OWN] = outbox[OWN]

    shared = []
    for zz in range(4):
        give = pl.ds(pl.multiple_of((2 * zz + 1 - link.core) * 512, 512), 512)
        shared.append(link.start(feats.at[:, give], other.at[:, pl.ds(512 * zz, 512)], dk=1))

    far = {}
    for h in (0, 1):
        a = axes[h][0]
        near[h, 1].wait_recv()
        far[h, 0] = link.start(code(h, 1, 0, 0, 32), code(h, 2, 0, 0, 32), **{a: -1})
        near[h, 3].wait_recv()
        far[h, 1] = link.start(code(h, 3, 0, 32, 32), code(h, 2, 0, 32, 32), **{a: 1})
    for h in (0, 1):
        spread(h, 1)

    top[...] = jnp.full(top.shape, LOW, F32)
    mass[...] = jnp.zeros(mass.shape, F32)
    last = {}

    def onward(f):
        for h in (0, 1):
            b = axes[h][1]
            step[h, f, 1].wait_recv()
            last[h, f, 0] = link.start(code(h, f, 1, 0, 32), code(h, f, 2, 0, 32), **{b: -1})
            step[h, f, 3].wait_recv()
            last[h, f, 1] = link.start(code(h, f, 3, 32, 32), code(h, f, 2, 32, 32), **{b: 1})

    def score(h, f):
        ids = [16 * h + 4 * s + f for s in range(4)]
        lhs = jnp.concatenate([codes[i] for i in ids], axis=0)
        s = inverse_temp * dot_nt(lhs, queries[...])
        for u, i in enumerate(ids):
            scores[i] = s[64 * u : 64 * u + 64] + bias_ref[i : i + 1]

        def part(j, carry):
            lanes = pl.ds(pl.multiple_of(256 * j, 256), 256)
            s = jnp.concatenate([scores[i, :, lanes] for i in ids], axis=0)
            before = top[:, lanes]
            after = jnp.maximum(before, jnp.max(s, axis=0, keepdims=True))
            mass[:, lanes] = mass[:, lanes] * jnp.exp(before - after) + jnp.sum(
                jnp.exp(s - after), axis=0, keepdims=True
            )
            top[:, lanes] = after
            return carry

        lax.fori_loop(0, 4, part, 0)

    for h in (0, 1):
        far[h, 0].wait_recv()
        far[h, 1].wait_recv()
        spread(h, 2)
    for h in (0, 1):
        spread(h, 3)
    q_in[1].wait_recv()
    q_far0 = link.start(q_rows(1, 0, 0, 64), q_rows(2, 0, 0, 64), dz=-1)
    s_in[1] = link.start(q_rows(1, 0), q_rows(1, 1), dk=1)
    q_in[3].wait_recv()
    q_far1 = link.start(q_rows(3, 0, 64, 64), q_rows(2, 0, 64, 64), dz=1)
    s_in[3] = link.start(q_rows(3, 0), q_rows(3, 1), dk=1)
    onward(0)
    onward(1)
    q_far0.wait_recv()
    q_far1.wait_recv()
    s_in[2] = link.start(q_rows(2, 0), q_rows(2, 1), dk=1)
    onward(2)
    for copy in shared:
        copy.wait_recv()
    for zz in range(4):
        keep = pl.ds(pl.multiple_of((2 * zz + link.core) * 512, 512), 512)
        rows = slice(512 * zz, 512 * zz + 512)
        turned[rows, 0:256] = feats[:, keep].T
        turned[rows, 256:512] = other[:, rows].T
    for copy in note_in.values():
        copy.wait_recv()
    for s in range(8):
        bias_ref[:, 128 * s : 128 * s + 128] = notes[s, 0:32]
        scale[:, 128 * s : 128 * s + 128] = inverse_temp * notes[s, 32:33]
    for dz in (0, 1, 3, 2):
        s_in[dz].wait_recv()
    for f in range(4):
        if f == 1:
            onward(3)
        for h in (0, 1):
            last[h, f, 0].wait_recv()
            last[h, f, 1].wait_recv()
            score(h, f)

    groups = [(slot(dz, dk), link.device(dz=dz, dk=dk)[0]) for dz, dk in LINE]
    for s, g in groups:
        mine[0, pl.ds(g, 1)] = top[:, 128 * s : 128 * s + 128]
        mine[1, pl.ds(g, 1)] = mass[:, 128 * s : 128 * s + 128]
    told = []
    for dz, dk in PEERS:
        told.append(link.start(mine, stats.at[slot(-dz, dk)], dz=dz, dk=dk))
    stats[OWN] = mine[...]
    for copy in told:
        copy.wait_recv()
    most = functools.reduce(jnp.maximum, [stats[r, 0] for r in range(8)])
    whole = sum(stats[r, 1] * jnp.exp(stats[r, 0] - most) for r in range(8))
    mine_lse[...] = most + jnp.log(whole)
    for s, g in groups:
        lanes = slice(128 * s, 128 * s + 128)
        shift[:, lanes] = mine_lse[pl.ds(g, 1)] - jnp.log(scale[:, lanes])

    def gradient(t):
        rows = pl.ds(256 * t, 256)

        def part(j, carry):
            lanes = pl.ds(pl.multiple_of(256 * j, 256), 256)
            s = scores[4 * t : 4 * t + 4, :, lanes].reshape(256, 256)
            grads[rows, lanes] = jnp.exp(s - shift[:, lanes]).astype(BF16)
            return carry

        lax.fori_loop(0, 4, part, 0)
        if t % 4 == 0:
            lanes = slice(128 * OWN, 128 * OWN + 128)
            own = slice(256 * t, 256 * t + 64)
            i = lax.broadcasted_iota(jnp.int32, (64, 128), 0) + 16 * t
            j = lax.broadcasted_iota(jnp.int32, (64, 128), 1)
            hit = jnp.where(i == j, scale[:, lanes], 0.0)
            grads[own, lanes] = (
                jnp.exp(scores[4 * t, :, lanes] - shift[:, lanes]) - hit
            ).astype(BF16)

    def to_codes(t):
        rows = pl.ds(256 * t, 256)
        dcode[rows] = jnp.dot(
            grads[rows], queries[...], preferred_element_type=F32
        ).astype(BF16)

    def backward(t):
        gradient(t)
        to_codes(t)

    def tile(h, t, at, n):
        return dcode.at[pl.ds(256 * (4 * h + t) + at, n)]

    back = {}
    for h in (0, 1):
        b = axes[h][1]
        backward(4 * h + 2)
        back[h, "p0"] = link.start(tile(h, 2, 0, 128), yp0.at[h], **{b: 1})
        back[h, "m0"] = link.start(tile(h, 2, 128, 128), ym0.at[h], **{b: -1})
    for h in (0, 1):
        b = axes[h][1]
        backward(4 * h + 1)
        back[h, "p1"] = link.start(tile(h, 1, 128, 128), yp1.at[h, pl.ds(128, 128)], **{b: 1})
        backward(4 * h + 3)
        back[h, "m1"] = link.start(tile(h, 3, 0, 128), ym1.at[h, pl.ds(0, 128)], **{b: -1})
    def relay(h):
        b = axes[h][1]
        back[h, "p0"].wait_recv()
        add_into(tile(h, 1, 0, 128), tile(h, 1, 0, 128)[...], yp0[h])
        back[h, "m0"].wait_recv()
        add_into(tile(h, 3, 128, 128), tile(h, 3, 128, 128)[...], ym0[h])
        for f in (1, 2, 0, 3):
            t, to, way = (1, yp1, 1) if f < 2 else (3, ym1, -1)
            back[h, "r", f] = link.start(
                tile(h, t, 64 * f, 64), to.at[h, pl.ds(64 * f, 64)], **{b: way}
            )

    gradient(0)
    gradient(4)
    home = {}

    def to_queries(dz):
        p = PLACE[dz]
        turn[...] = grads[:, 256 * p : 256 * p + 256].T
        dquery[256 * p : 256 * p + 256] = jnp.dot(
            turn[...], codes[...].reshape(2048, width), preferred_element_type=F32
        ).astype(BF16)
        home[dz] = link.start(dquery.at[pl.ds(256 * p + 128, 128)], sib.at[p], dk=1)

    def dq(dz, at=0, n=128):
        return dquery.at[pl.ds(128 * slot(dz, 0) + at, n)]

    def add_sibling(dz):
        home[dz].wait_recv()
        add_into(dq(dz), dq(dz)[...], sib[PLACE[dz]])

    to_queries(2)
    to_queries(1)
    to_queries(3)
    add_sibling(2)
    z0p = link.start(dq(2, 0, 64), zp0, dz=1)
    z0m = link.start(dq(2, 64, 64), zm0, dz=-1)
    add_sibling(1)
    z1p = link.start(dq(1, 64, 64), zp1.at[pl.ds(64, 64)], dz=1)
    relay(0)
    relay(1)
    add_sibling(3)
    z1m = link.start(dq(3, 0, 64), zm1.at[pl.ds(0, 64)], dz=-1)
    to_queries(0)
    to_codes(0)
    to_codes(4)

    def inner(h, f):
        a = axes[h][0]
        if f == 2:
            for name in ("p1", "m1"):
                back[h, name].wait_recv()
        low = (low_a, low_b)[h]
        back[h, "r", f].wait_recv()
        s = slice(64 * f, 64 * f + 64)
        total = (
            tile(h, 0, 64 * f, 64)[...].astype(F32)
            + yp1[h, s].astype(F32)
            + ym1[h, s].astype(F32)
        )
        if f == 0:
            dc_sum[64 * h : 64 * h + 64] = total
        else:
            low[s] = total.astype(BF16)
        if f == 2:
            back[h, "q0"] = link.start(low.at[pl.ds(128, 32)], xp0.at[h], **{a: 1})
            back[h, "n0"] = link.start(low.at[pl.ds(160, 32)], xm0.at[h], **{a: -1})
        if f == 1:
            back[h, "q1"] = link.start(low.at[pl.ds(96, 32)], xp1.at[h, pl.ds(32, 32)], **{a: 1})
        if f == 3:
            back[h, "n1"] = link.start(low.at[pl.ds(192, 32)], xm1.at[h, pl.ds(0, 32)], **{a: -1})

    def outer(h):
        a = axes[h][0]
        low = (low_a, low_b)[h]
        back[h, "q0"].wait_recv()
        add_into(low.at[pl.ds(64, 32)], low[64:96], xp0[h])
        back[h, "q2"] = link.start(low.at[pl.ds(64, 32)], xp1.at[h, pl.ds(0, 32)], **{a: 1})
        back[h, "n0"].wait_recv()
        add_into(low.at[pl.ds(224, 32)], low[224:256], xm0[h])
        back[h, "n2"] = link.start(low.at[pl.ds(224, 32)], xm1.at[h, pl.ds(32, 32)], **{a: -1})

    z0p.wait_recv()
    add_into(dq(1, 0, 64), dq(1, 0, 64)[...], zp0[...])
    z2p = link.start(dq(1, 0, 64), zp1.at[pl.ds(0, 64)], dz=1)
    z0m.wait_recv()
    add_into(dq(3, 64, 64), dq(3, 64, 64)[...], zm0[...])
    z2m = link.start(dq(3, 64, 64), zm1.at[pl.ds(64, 64)], dz=-1)
    for f in (2, 1, 3, 0):
        for h in (0, 1):
            inner(h, f)
    outer(0)
    outer(1)
    home[0].wait_recv()
    for copy in (z1p, z2p, z1m, z2m):
        copy.wait_recv()
    d_q = (
        dq(0)[...].astype(F32)
        + sib[PLACE[0]].astype(F32)
        + zp1[...].astype(F32)
        + zm1[...].astype(F32)
    )
    dz_ref[0:128] = norm_back(d_q, unit[0:128], inverse[0:128])
    pair_q = link.start(dz_ref.at[pl.ds(0, 128)], dz_ref.at[pl.ds(256, 128)], dk=1)
    for h in (0, 1):
        for name in ("q1", "q2", "n1", "n2"):
            back[h, name].wait_recv()
        s = slice(64 * h, 64 * h + 64)
        dc_sum[s] = dc_sum[s] + xp1[h].astype(F32) + xm1[h].astype(F32)
    dz_ref[128:256] = norm_back(dc_sum[...], unit[128:256], inverse[128:256])
    pair_c = link.start(dz_ref.at[pl.ds(128, 128)], dz_ref.at[pl.ds(384, 128)], dk=1)
    pair_q.wait_recv()
    pair_c.wait_recv()
    here = {"x": link.x, "y": link.y, "z": link.z}
    per = len(boxes) // len(PARTS)
    low, high = pl.ds(0, 2), pl.ds(2, 2)

    class Part:
        def __init__(self, i):
            self.at, self.n, self.order = PARTS[i]
            self.boxes = boxes[per * i : per * i + per]
            self.left = "zxy"
            self.level = 0
            self.value = partial[i]

        def chunk(self, d, half=slice(None)):
            axis = self.order[self.level]
            index, rest = [], [half]
            for a in self.left:
                if a == axis:
                    index.append((here[a] + d) % 4)
                else:
                    index.append(rest.pop() if rest else slice(None))
            return self.value.at[tuple(index)]

        def box(self, name):
            if self.level == 0:
                return self.boxes[("p0", "m0", "p1", "m1", "sum").index(name)]
            return self.boxes[1 + 4 * self.level + ("p1", "m1", "far", "sum").index(name)]

        def rows_of(self, ref, half):
            return ref.at[half]

        def open(self, which=(2, 1, 3)):
            name = "d" + self.order[self.level]
            if 2 in which:
                self.c = {}
            if self.level:
                for d, key in ((2, "far"), (1, "p1"), (3, "m1")):
                    self.c[key] = link.start(self.chunk(d), self.box(key), **{name: d})
                return
            if 2 in which:
                self.c["p0"] = link.start(self.chunk(2, low), self.box("p0"), **{name: 1})
                self.c["m0"] = link.start(self.chunk(2, high), self.box("m0"), **{name: -1})
            if 1 in which:
                self.c["p1"] = link.start(
                    self.chunk(1, high), self.rows_of(self.box("p1"), high), **{name: 1}
                )
            if 3 in which:
                self.c["m1"] = link.start(
                    self.chunk(3, low), self.rows_of(self.box("m1"), low), **{name: -1}
                )

        def merge(self, dst, *terms):
            if len(dst.shape) <= 2:
                add_into(dst, *[t[...] for t in terms])
                return

            def body(i, carry):
                add_into(dst.at[i], *[t[i] for t in terms])
                return carry

            lax.fori_loop(0, dst.shape[0], body, 0)

        def relay(self):
            name = "d" + self.order[self.level]
            self.c["p0"].wait_recv()
            self.merge(self.chunk(1, low), self.chunk(1, low), self.box("p0"))
            self.c["p2"] = link.start(
                self.chunk(1, low), self.rows_of(self.box("p1"), low), **{name: 1}
            )
            self.c["m0"].wait_recv()
            self.merge(self.chunk(3, high), self.chunk(3, high), self.box("m0"))
            self.c["m2"] = link.start(
                self.chunk(3, high), self.rows_of(self.box("m1"), high), **{name: -1}
            )

        def close(self):
            for key, copy in self.c.items():
                if key not in ("p0", "m0"):
                    copy.wait_recv()
            terms = [self.chunk(0), self.box("p1"), self.box("m1")]
            if self.level:
                terms.append(self.box("far"))
            if self.level == 2:
                total = sum(t[...].astype(F32) for t in terms)
                pg_ref[:, self.at : self.at + self.n] = total
                return
            done = self.box("sum")
            self.merge(done, *terms)
            self.value = done
            self.left = self.left.replace(self.order[self.level], "")
            self.level += 1

    parts = [Part(i) for i in range(len(PARTS))]
    for d in (2, 1, 3, 0):
        at = (link.z + d) % 4
        rows = pl.ds(pl.multiple_of(512 * at, 512), 512)
        value = jnp.dot(turned[rows], dz_ref[:, 0:384], preferred_element_type=F32)
        value = value.astype(BF16).reshape(4, 4, 32, 384)
        partial[0][at] = value[:, :, :, 0:256]
        partial[1][at] = value[:, :, :, 256:384]
        if d:
            parts[0].open((d,))
    parts[1].open((2,))
    for i in (2, 4):
        at, n = parts[i].at, parts[i].n + parts[i + 1].n
        value = jnp.dot(turned[...], dz_ref[:, at : at + n], preferred_element_type=F32)
        value = value.astype(BF16).reshape(4, 4, 4, 32, n)
        partial[i][...] = value[..., 0 : parts[i].n]
        partial[i + 1][...] = value[..., parts[i].n :]
        parts[i].open()
        parts[i + 1].open((2,))

    puts = []

    def features(i):
        rows = slice(1024 * i, 1024 * i + 1024)
        fgrads[:, rows] = dot_nt(dz_ref[0:256], weights[rows]).astype(BF16)
        for n, hbm in enumerate((qg_hbm, cg_hbm)):
            put = pltpu.make_async_copy(
                fgrads.at[pl.ds(128 * n, 128), pl.ds(1024 * i, 1024)],
                hbm.at[:, pl.ds(1024 * i, 1024)],
                local.at[4 + 2 * i + n],
            )
            put.start()
            puts.append(put)

    features(0)
    for i in (0, 4, 2):
        parts[i].relay()
        parts[i + 1].open((1, 3))
        if i != 2:
            features(1 + i // 4)
    for i in (1, 5, 3):
        parts[i].relay()
    features(3)
    order = [parts[i] for i in (4, 0, 2, 5, 1, 3)]
    for level in range(3):
        for part in order:
            part.close()
            if level < 2:
                part.open()
    for put in puts:
        put.wait()
    link.drain()


def place(q_in, c_in, p_in, q_out, c_out, p_out, q_held, c_held, p_held, come, leave):
    width = q_held.shape[1] // 4
    pairs = [(p_in, p_held, p_out)]
    for i in range(4):
        cols = pl.ds(width * i, width)
        pairs.append((q_in.at[:, cols], q_held.at[:, cols], q_out.at[:, cols]))
        pairs.append((c_in.at[:, cols], c_held.at[:, cols], c_out.at[:, cols]))
    first = [pltpu.make_async_copy(a, b, come.at[i]) for i, (a, b, _) in enumerate(pairs)]
    second = [pltpu.make_async_copy(b, c, leave.at[i]) for i, (_, b, c) in enumerate(pairs)]
    for copy in first:
        copy.start()
    for copy, onward in zip(first, second):
        copy.wait()
        onward.start()
    for copy in second:
        copy.wait()


def body(query_feat, code_feat, projection, hard_ids, loss_weight):
    rows, depth = query_feat.shape
    width = projection.shape[1]
    vmem = pl.BlockSpec(memory_space=pltpu.VMEM)
    anywhere = pl.BlockSpec(memory_space=pl.ANY)

    def vm(*shape, dtype=BF16):
        return pltpu.VMEM(shape, dtype)

    boxes = []
    for _, n, _ in PARTS:
        boxes += [vm(2, 4, 32, n)] * 2 + [vm(4, 4, 32, n)] * 3
        boxes += [vm(4, 32, n)] * 4 + [vm(32, n)] * 4
    outs = (
        jax.ShapeDtypeStruct((rows, depth), BF16),
        jax.ShapeDtypeStruct((rows, depth), BF16),
        jax.ShapeDtypeStruct((depth // 128, width), F32),
    )
    made = pl.pallas_call(
        step,
        out_shape=outs,
        in_specs=[anywhere] * 3 + [pl.BlockSpec(memory_space=pltpu.SMEM), vmem],
        out_specs=(anywhere, anywhere, vmem),
        scratch_shapes=[
            vm(256, depth),
            vm(8, 40, 128, dtype=F32),
            vm(32, 1024, dtype=F32),
            vm(depth, width),
            vm(256, depth),
            vm(256, depth // 2),
            vm(depth // 2, 512),
            vm(256, width, dtype=F32),
            vm(256, 1, dtype=F32),
            vm(512, width),
            vm(1024, width),
            vm(32, 64, width),
            vm(32, 64, 1024, dtype=F32),
            vm(2048, 1024),
            vm(256, 2048),
            vm(2048, width),
            vm(1024, width),
            vm(8, 40, 128, dtype=F32),
            vm(2, 8, 128, dtype=F32),
            vm(8, 128, dtype=F32),
            vm(8, 2, 8, 128, dtype=F32),
            vm(1, 1024, dtype=F32),
            vm(1, 1024, dtype=F32),
            vm(1, 1024, dtype=F32),
            vm(1, 1024, dtype=F32),
            vm(2, 128, width),
            vm(2, 128, width),
            vm(2, 256, width),
            vm(2, 256, width),
            vm(2, 32, width),
            vm(2, 32, width),
            vm(2, 64, width),
            vm(2, 64, width),
            vm(4, 128, width),
            vm(64, width),
            vm(64, width),
            vm(128, width),
            vm(128, width),
            vm(256, width),
            vm(256, width),
            vm(128, width, dtype=F32),
            *[vm(4, 4, 4, 32, n) for _, n, _ in PARTS],
            *boxes,
            pltpu.SemaphoreType.DMA((N_COPIES,)),
            pltpu.SemaphoreType.DMA((N_COPIES,)),
            pltpu.SemaphoreType.DMA((12,)),
        ],
        compiler_params=pltpu.CompilerParams(
            collective_id=0, has_side_effects=True, vmem_limit_bytes=60 * 2**20
        ),
        name="step",
    )(query_feat, code_feat, projection, hard_ids, loss_weight[None])
    return tuple(
        pl.pallas_call(
            place,
            out_shape=outs,
            in_specs=[anywhere] * 3,
            out_specs=(anywhere,) * 3,
            scratch_shapes=[
                vm(rows, depth),
                vm(rows, depth),
                vm(depth // 128, width, dtype=F32),
                pltpu.SemaphoreType.DMA((9,)),
                pltpu.SemaphoreType.DMA((9,)),
            ],
            name="place",
        )(*made)
    )


def solution(mesh):
    lined = P(("group", "member"), None)
    return jax.shard_map(
        body,
        mesh=mesh,
        in_specs=(lined, lined, P(), lined, P(("group", "member"))),
        out_specs=(lined, lined, lined),
        check_vma=False,
    )
```

```python
import functools

import jax
import jax.numpy as jnp
from jax import lax
from jax.experimental import pallas as pl
from jax.experimental.pallas import tpu as pltpu
from jax.sharding import PartitionSpec as P

MESH = pl.DeviceIdType.MESH
F32 = jnp.float32
BF16 = jnp.bfloat16
inverse_temp = 120.0
epsilon = 1e-06
LOW = -1e30

PLACE = {2: 0, 1: 1, 3: 2, 0: 3}
LINE = [(dz, dk) for dz in (2, 1, 3, 0) for dk in (0, 1)]
PEERS = [p for p in LINE if p != (0, 0)]


def slot(dz, dk):
    return 2 * PLACE[dz % 4] + dk % 2


OWN = slot(0, 0)


class Links:
    def __init__(self, send, recv):
        self.send, self.recv, self.made, self.left = send, recv, [], 0
        group, member = lax.axis_index("group"), lax.axis_index("member")
        self.z, self.core = group // 2, group % 2
        self.x, self.y = member // 4, member % 4

    def device(self, dx=0, dy=0, dz=0, dk=0):
        group = 2 * ((self.z + dz % 4) % 4) + (self.core + dk) % 2
        member = 4 * ((self.x + dx % 4) % 4) + (self.y + dy % 4) % 4
        return (group, member)

    def start(self, src, dst, **where):
        i = len(self.made)
        copy = pltpu.make_async_remote_copy(
            src_ref=src,
            dst_ref=dst,
            send_sem=self.send.at[i],
            recv_sem=self.recv.at[i],
            device_id=self.device(**where),
            device_id_type=MESH,
        )
        copy.start()
        self.made.append(copy)
        return copy

    def greet(self):
        sem = pltpu.get_barrier_semaphore()
        places = [dict(dx=1), dict(dx=-1), dict(dy=1), dict(dy=-1)]
        places += [dict(dz=dz, dk=dk) for dz, dk in PEERS]
        for where in places:
            pl.semaphore_signal(sem, inc=1, device_id=self.device(**where), device_id_type=MESH)

    def meet(self):
        pl.semaphore_wait(pltpu.get_barrier_semaphore(), 4 + len(PEERS))

    def drain(self, upto=None):
        upto = len(self.made) if upto is None else upto
        for copy in self.made[self.left : upto]:
            copy.wait_send()
        self.left = upto


def dot_nt(a, b):
    return lax.dot_general(a, b, (((1,), (1,)), ((), ())), preferred_element_type=F32)


def add_into(dst, *terms):
    total = terms[0].astype(F32)
    for term in terms[1:]:
        total = total + term.astype(F32)
    dst[...] = total.astype(dst.dtype)


def norm_back(upstream, unit, inverse):
    inner = jnp.sum(unit * upstream, axis=1, keepdims=True)
    return (inverse * (upstream - unit * inner)).astype(BF16)


PARTS = (
    (0, 256, "zxy"),
    (256, 128, "zxy"),
    (384, 256, "xyz"),
    (640, 128, "xyz"),
    (768, 128, "yzx"),
    (896, 128, "yzx"),
)

N_COPIES = 7 + 4 + 3 + 16 + 4 + 4 + 2 + 3 + 16 + 7 + 12 + 4 + 6 + 12 + 2 + 4 + 72


def step(
    qf_hbm, cf_hbm, w_hbm, ids_ref, weight_ref,
    qg_hbm, cg_hbm, pg_ref,
    fgrads, outbox, bias_ref, weights, feats, other, turned, unit, inverse, dz_ref,
    queries, codes, scores, grads, turn, dcode, dquery, notes, mine, mine_lse, stats, top, mass, shift, scale,
    yp0, ym0, yp1, ym1, xp0, xm0, xp1, xm1, sib, zp0, zm0, zp1, zm1, low_a, low_b, dc_sum,
    *rest,
):
    boxes, (send, recv, local) = rest[:-3], rest[-3:]
    partial, boxes = boxes[: len(PARTS)], boxes[len(PARTS) :]
    width = weights.shape[1]
    link = Links(send, recv)
    loads = [
        pltpu.make_async_copy(f, feats.at[pl.ds(128 * i, 128)], local.at[i])
        for i, f in enumerate((qf_hbm, cf_hbm))
    ]
    fetch = [
        pltpu.make_async_copy(
            w_hbm.at[:, pl.ds(512 * n, 512)], weights.at[:, pl.ds(512 * n, 512)], local.at[2 + n]
        )
        for n in range(2)
    ]
    for load in (loads[1], *fetch, loads[0]):
        load.start()
    link.greet()

    row = lax.broadcasted_iota(jnp.int32, (32, 128), 0)
    first, second, half = row % 4, (row // 4) % 4, row // 16
    ax = (link.x + jnp.where(half == 0, first, second)) % 4
    ay = (link.y + jnp.where(half == 0, second, first)) % 4
    block = (4 * ax + ay) * 2 + half
    for dz, dk in LINE:
        if (dz, dk) == (0, 0):
            bias = jnp.zeros((32, 128), F32)
        else:
            base = 32 * (2 * ((link.z + dz) % 4) + (link.core + dk) % 2)
            bias = jnp.full((32, 128), LOW, F32)
            for i in range(ids_ref.shape[1]):
                bias = jnp.where(block == ids_ref[0, i] - base, 0.0, bias)
        outbox[slot(dz, dk), 0:32] = bias
        outbox[slot(dz, dk), 32:40] = jnp.broadcast_to(weight_ref[...], (8, 128))

    def embed(rows, waits=()):
        for n in range(2):
            if waits:
                waits[n].wait()
            cols = slice(512 * n, 512 * n + 512)
            unit[rows, cols] = jnp.dot(
                feats[rows], weights[:, cols], preferred_element_type=F32
            )
        values = unit[rows]
        inverse[rows] = lax.rsqrt(jnp.sum(values * values, axis=1, keepdims=True) + epsilon)
        unit[rows] = unit[rows] * inverse[rows]

    loads[1].wait()
    embed(slice(128, 256), fetch)
    loads[0].wait()
    link.meet()

    def q_rows(dz, dk, at=0, n=128):
        return queries.at[pl.ds(128 * slot(dz, dk) + at, n)]

    def code(half, first, second, at=0, n=64):
        return codes.at[16 * half + 4 * second + first, pl.ds(at, n)]

    axes = (("dx", "dy"), ("dy", "dx"))

    codes[0] = unit[128:192].astype(BF16)
    codes[16] = unit[192:256].astype(BF16)
    near = {}
    for h in (0, 1):
        a = axes[h][0]
        near[h, 3] = link.start(code(h, 0, 0), code(h, 3, 0), **{a: 1})
        near[h, 1] = link.start(code(h, 0, 0), code(h, 1, 0), **{a: -1})
    step = {}

    def spread(h, f):
        b = axes[h][1]
        step[h, f, 3] = link.start(code(h, f, 0), code(h, f, 3), **{b: 1})
        step[h, f, 1] = link.start(code(h, f, 0), code(h, f, 1), **{b: -1})

    for h in (0, 1):
        spread(h, 0)
    embed(slice(0, 128))
    queries[pl.ds(128 * OWN, 128)] = unit[0:128].astype(BF16)
    q_in = {}
    q_in[3] = link.start(q_rows(0, 0), q_rows(3, 0), dz=1)
    q_in[1] = link.start(q_rows(0, 0), q_rows(1, 0), dz=-1)
    s_in = {0: link.start(q_rows(0, 0), q_rows(0, 1), dk=1)}
    note_in = {}
    for dz, dk in PEERS:
        s, r = slot(dz, dk), slot(-dz, dk)
        note_in[r] = link.start(outbox.at[s], notes.at[r], dz=dz, dk=dk)
    notes[OWN] = outbox[OWN]

    shared = []
    for zz in range(4):
        give = pl.ds(pl.multiple_of((2 * zz + 1 - link.core) * 512, 512), 512)
        shared.append(link.start(feats.at[:, give], other.at[:, pl.ds(512 * zz, 512)], dk=1))

    far = {}
    for h in (0, 1):
        a = axes[h][0]
        near[h, 1].wait_recv()
        far[h, 0] = link.start(code(h, 1, 0, 0, 32), code(h, 2, 0, 0, 32), **{a: -1})
        near[h, 3].wait_recv()
        far[h, 1] = link.start(code(h, 3, 0, 32, 32), code(h, 2, 0, 32, 32), **{a: 1})
    for h in (0, 1):
        spread(h, 1)

    top[...] = jnp.full(top.shape, LOW, F32)
    mass[...] = jnp.zeros(mass.shape, F32)
    last = {}

    def onward(f):
        for h in (0, 1):
            b = axes[h][1]
            step[h, f, 1].wait_recv()
            last[h, f, 0] = link.start(code(h, f, 1, 0, 32), code(h, f, 2, 0, 32), **{b: -1})
            step[h, f, 3].wait_recv()
            last[h, f, 1] = link.start(code(h, f, 3, 32, 32), code(h, f, 2, 32, 32), **{b: 1})

    def score(ids):
        lhs = jnp.concatenate([codes[i] for i in ids], axis=0)
        s = inverse_temp * dot_nt(lhs, queries[...])
        for u, i in enumerate(ids):
            scores[i] = s[64 * u : 64 * u + 64] + bias_ref[i : i + 1]

        def part(j, carry):
            lanes = pl.ds(pl.multiple_of(256 * j, 256), 256)
            s = jnp.concatenate([scores[i, :, lanes] for i in ids], axis=0)
            before = top[:, lanes]
            after = jnp.maximum(before, jnp.max(s, axis=0, keepdims=True))
            mass[:, lanes] = mass[:, lanes] * jnp.exp(before - after) + jnp.sum(
                jnp.exp(s - after), axis=0, keepdims=True
            )
            top[:, lanes] = after
            return carry

        lax.fori_loop(0, 4, part, 0)

    for h in (0, 1):
        far[h, 0].wait_recv()
        far[h, 1].wait_recv()
        spread(h, 2)
    for h in (0, 1):
        spread(h, 3)
    q_in[1].wait_recv()
    q_far0 = link.start(q_rows(1, 0, 0, 64), q_rows(2, 0, 0, 64), dz=-1)
    s_in[1] = link.start(q_rows(1, 0), q_rows(1, 1), dk=1)
    q_in[3].wait_recv()
    q_far1 = link.start(q_rows(3, 0, 64, 64), q_rows(2, 0, 64, 64), dz=1)
    s_in[3] = link.start(q_rows(3, 0), q_rows(3, 1), dk=1)
    onward(0)
    onward(1)
    q_far0.wait_recv()
    q_far1.wait_recv()
    s_in[2] = link.start(q_rows(2, 0), q_rows(2, 1), dk=1)
    onward(2)
    for copy in shared:
        copy.wait_recv()
    for zz in range(4):
        keep = pl.ds(pl.multiple_of((2 * zz + link.core) * 512, 512), 512)
        rows = slice(512 * zz, 512 * zz + 512)
        turned[rows, 0:256] = feats[:, keep].T
        turned[rows, 256:512] = other[:, rows].T
    for copy in note_in.values():
        copy.wait_recv()
    for s in range(8):
        bias_ref[:, 128 * s : 128 * s + 128] = notes[s, 0:32]
        scale[:, 128 * s : 128 * s + 128] = inverse_temp * notes[s, 32:33]
    for dz in (0, 1, 3, 2):
        s_in[dz].wait_recv()
    def blocks(h, f, seconds=(0, 1, 2, 3)):
        return [16 * h + 4 * s + f for s in seconds]

    def finish_row(h, f):
        last[h, f, 0].wait_recv()
        last[h, f, 1].wait_recv()

    for f in range(3):
        if f == 1:
            onward(3)
        for h in (0, 1):
            finish_row(h, f)
            score(blocks(h, f))
    score(blocks(0, 3, (0, 1, 3)) + blocks(1, 3, (0, 1, 3)))
    finish_row(0, 3)
    finish_row(1, 3)
    score(blocks(0, 3, (2,)) + blocks(1, 3, (2,)))

    groups = [(slot(dz, dk), link.device(dz=dz, dk=dk)[0]) for dz, dk in LINE]
    for s, g in groups:
        mine[0, pl.ds(g, 1)] = top[:, 128 * s : 128 * s + 128]
        mine[1, pl.ds(g, 1)] = mass[:, 128 * s : 128 * s + 128]
    told = []
    for dz, dk in PEERS:
        told.append(link.start(mine, stats.at[slot(-dz, dk)], dz=dz, dk=dk))
    stats[OWN] = mine[...]
    for copy in told:
        copy.wait_recv()
    most = functools.reduce(jnp.maximum, [stats[r, 0] for r in range(8)])
    whole = sum(stats[r, 1] * jnp.exp(stats[r, 0] - most) for r in range(8))
    mine_lse[...] = most + jnp.log(whole)
    for s, g in groups:
        lanes = slice(128 * s, 128 * s + 128)
        shift[:, lanes] = mine_lse[pl.ds(g, 1)] - jnp.log(scale[:, lanes])

    def gradient(t):
        rows = pl.ds(256 * t, 256)

        def part(j, carry):
            lanes = pl.ds(pl.multiple_of(256 * j, 256), 256)
            s = scores[4 * t : 4 * t + 4, :, lanes].reshape(256, 256)
            grads[rows, lanes] = jnp.exp(s - shift[:, lanes]).astype(BF16)
            return carry

        lax.fori_loop(0, 4, part, 0)
        if t % 4 == 0:
            lanes = slice(128 * OWN, 128 * OWN + 128)
            own = slice(256 * t, 256 * t + 64)
            i = lax.broadcasted_iota(jnp.int32, (64, 128), 0) + 16 * t
            j = lax.broadcasted_iota(jnp.int32, (64, 128), 1)
            hit = jnp.where(i == j, scale[:, lanes], 0.0)
            grads[own, lanes] = (
                jnp.exp(scores[4 * t, :, lanes] - shift[:, lanes]) - hit
            ).astype(BF16)

    def to_codes(t):
        rows = pl.ds(256 * t, 256)
        dcode[rows] = jnp.dot(
            grads[rows], queries[...], preferred_element_type=F32
        ).astype(BF16)

    def backward(t):
        gradient(t)
        to_codes(t)

    def tile(h, t, at, n):
        return dcode.at[pl.ds(256 * (4 * h + t) + at, n)]

    back = {}
    for h in (0, 1):
        b = axes[h][1]
        backward(4 * h + 2)
        back[h, "p0"] = link.start(tile(h, 2, 0, 128), yp0.at[h], **{b: 1})
        back[h, "m0"] = link.start(tile(h, 2, 128, 128), ym0.at[h], **{b: -1})
    for h in (0, 1):
        b = axes[h][1]
        backward(4 * h + 1)
        back[h, "p1"] = link.start(tile(h, 1, 128, 128), yp1.at[h, pl.ds(128, 128)], **{b: 1})
        backward(4 * h + 3)
        back[h, "m1"] = link.start(tile(h, 3, 0, 128), ym1.at[h, pl.ds(0, 128)], **{b: -1})
    def relay(h):
        b = axes[h][1]
        back[h, "p0"].wait_recv()
        add_into(tile(h, 1, 0, 128), tile(h, 1, 0, 128)[...], yp0[h])
        back[h, "m0"].wait_recv()
        add_into(tile(h, 3, 128, 128), tile(h, 3, 128, 128)[...], ym0[h])
        for f in (1, 2, 0, 3):
            t, to, way = (1, yp1, 1) if f < 2 else (3, ym1, -1)
            back[h, "r", f] = link.start(
                tile(h, t, 64 * f, 64), to.at[h, pl.ds(64 * f, 64)], **{b: way}
            )

    gradient(0)
    gradient(4)
    home = {}

    def to_queries(dz):
        p = PLACE[dz]
        turn[...] = grads[:, 256 * p : 256 * p + 256].T
        dquery[256 * p : 256 * p + 256] = jnp.dot(
            turn[...], codes[...].reshape(2048, width), preferred_element_type=F32
        ).astype(BF16)
        home[dz] = link.start(dquery.at[pl.ds(256 * p + 128, 128)], sib.at[p], dk=1)

    def dq(dz, at=0, n=128):
        return dquery.at[pl.ds(128 * slot(dz, 0) + at, n)]

    def add_sibling(dz):
        home[dz].wait_recv()
        add_into(dq(dz), dq(dz)[...], sib[PLACE[dz]])

    to_queries(2)
    to_queries(1)
    relay(0)
    relay(1)
    add_sibling(2)
    z0p = link.start(dq(2, 0, 64), zp0, dz=1)
    z0m = link.start(dq(2, 64, 64), zm0, dz=-1)
    add_sibling(1)
    z1p = link.start(dq(1, 64, 64), zp1.at[pl.ds(64, 64)], dz=1)
    to_queries(3)
    to_queries(0)
    add_sibling(3)
    z1m = link.start(dq(3, 0, 64), zm1.at[pl.ds(0, 64)], dz=-1)
    to_codes(0)
    to_codes(4)

    def inner(h, f):
        a = axes[h][0]
        if f == 2:
            for name in ("p1", "m1"):
                back[h, name].wait_recv()
        low = (low_a, low_b)[h]
        back[h, "r", f].wait_recv()
        s = slice(64 * f, 64 * f + 64)
        total = (
            tile(h, 0, 64 * f, 64)[...].astype(F32)
            + yp1[h, s].astype(F32)
            + ym1[h, s].astype(F32)
        )
        if f == 0:
            dc_sum[64 * h : 64 * h + 64] = total
        else:
            low[s] = total.astype(BF16)
        if f == 2:
            back[h, "q0"] = link.start(low.at[pl.ds(128, 32)], xp0.at[h], **{a: 1})
            back[h, "n0"] = link.start(low.at[pl.ds(160, 32)], xm0.at[h], **{a: -1})
        if f == 1:
            back[h, "q1"] = link.start(low.at[pl.ds(96, 32)], xp1.at[h, pl.ds(32, 32)], **{a: 1})
        if f == 3:
            back[h, "n1"] = link.start(low.at[pl.ds(192, 32)], xm1.at[h, pl.ds(0, 32)], **{a: -1})

    def outer(h):
        a = axes[h][0]
        low = (low_a, low_b)[h]
        back[h, "q0"].wait_recv()
        add_into(low.at[pl.ds(64, 32)], low[64:96], xp0[h])
        back[h, "q2"] = link.start(low.at[pl.ds(64, 32)], xp1.at[h, pl.ds(0, 32)], **{a: 1})
        back[h, "n0"].wait_recv()
        add_into(low.at[pl.ds(224, 32)], low[224:256], xm0[h])
        back[h, "n2"] = link.start(low.at[pl.ds(224, 32)], xm1.at[h, pl.ds(32, 32)], **{a: -1})

    z0p.wait_recv()
    add_into(dq(1, 0, 64), dq(1, 0, 64)[...], zp0[...])
    z2p = link.start(dq(1, 0, 64), zp1.at[pl.ds(0, 64)], dz=1)
    z0m.wait_recv()
    add_into(dq(3, 64, 64), dq(3, 64, 64)[...], zm0[...])
    z2m = link.start(dq(3, 64, 64), zm1.at[pl.ds(64, 64)], dz=-1)
    for f in (2, 1, 3, 0):
        for h in (0, 1):
            inner(h, f)
    outer(0)
    outer(1)
    home[0].wait_recv()
    for copy in (z1p, z2p, z1m, z2m):
        copy.wait_recv()
    d_q = (
        dq(0)[...].astype(F32)
        + sib[PLACE[0]].astype(F32)
        + zp1[...].astype(F32)
        + zm1[...].astype(F32)
    )
    dz_ref[0:128] = norm_back(d_q, unit[0:128], inverse[0:128])
    pair_q = link.start(dz_ref.at[pl.ds(0, 128)], dz_ref.at[pl.ds(256, 128)], dk=1)
    for h in (0, 1):
        for name in ("q1", "q2", "n1", "n2"):
            back[h, name].wait_recv()
        s = slice(64 * h, 64 * h + 64)
        dc_sum[s] = dc_sum[s] + xp1[h].astype(F32) + xm1[h].astype(F32)
    dz_ref[128:256] = norm_back(dc_sum[...], unit[128:256], inverse[128:256])
    pair_c = link.start(dz_ref.at[pl.ds(128, 128)], dz_ref.at[pl.ds(384, 128)], dk=1)
    pair_q.wait_recv()
    pair_c.wait_recv()
    here = {"x": link.x, "y": link.y, "z": link.z}
    per = len(boxes) // len(PARTS)
    low, high = pl.ds(0, 2), pl.ds(2, 2)

    class Part:
        def __init__(self, i):
            self.at, self.n, self.order = PARTS[i]
            self.boxes = boxes[per * i : per * i + per]
            self.left = "zxy"
            self.level = 0
            self.value = partial[i]

        def chunk(self, d, half=slice(None)):
            axis = self.order[self.level]
            index, rest = [], [half]
            for a in self.left:
                if a == axis:
                    index.append((here[a] + d) % 4)
                else:
                    index.append(rest.pop() if rest else slice(None))
            return self.value.at[tuple(index)]

        def box(self, name):
            if self.level == 0:
                return self.boxes[("p0", "m0", "p1", "m1", "sum").index(name)]
            return self.boxes[1 + 4 * self.level + ("p1", "m1", "far", "sum").index(name)]

        def rows_of(self, ref, half):
            return ref.at[half]

        def open(self, which=(2, 1, 3)):
            name = "d" + self.order[self.level]
            if 2 in which:
                self.c = {}
            if self.level:
                for d, key in ((2, "far"), (1, "p1"), (3, "m1")):
                    self.c[key] = link.start(self.chunk(d), self.box(key), **{name: d})
                return
            if 2 in which:
                self.c["p0"] = link.start(self.chunk(2, low), self.box("p0"), **{name: 1})
                self.c["m0"] = link.start(self.chunk(2, high), self.box("m0"), **{name: -1})
            if 1 in which:
                self.c["p1"] = link.start(
                    self.chunk(1, high), self.rows_of(self.box("p1"), high), **{name: 1}
                )
            if 3 in which:
                self.c["m1"] = link.start(
                    self.chunk(3, low), self.rows_of(self.box("m1"), low), **{name: -1}
                )

        def merge(self, dst, *terms):
            if len(dst.shape) <= 2:
                add_into(dst, *[t[...] for t in terms])
                return

            def body(i, carry):
                add_into(dst.at[i], *[t[i] for t in terms])
                return carry

            lax.fori_loop(0, dst.shape[0], body, 0)

        def relay(self):
            name = "d" + self.order[self.level]
            self.c["p0"].wait_recv()
            self.merge(self.chunk(1, low), self.chunk(1, low), self.box("p0"))
            self.c["p2"] = link.start(
                self.chunk(1, low), self.rows_of(self.box("p1"), low), **{name: 1}
            )
            self.c["m0"].wait_recv()
            self.merge(self.chunk(3, high), self.chunk(3, high), self.box("m0"))
            self.c["m2"] = link.start(
                self.chunk(3, high), self.rows_of(self.box("m1"), high), **{name: -1}
            )

        def close(self):
            for key, copy in self.c.items():
                if key not in ("p0", "m0"):
                    copy.wait_recv()
            terms = [self.chunk(0), self.box("p1"), self.box("m1")]
            if self.level:
                terms.append(self.box("far"))
            if self.level == 2:
                total = sum(t[...].astype(F32) for t in terms)
                pg_ref[:, self.at : self.at + self.n] = total
                return
            done = self.box("sum")
            self.merge(done, *terms)
            self.value = done
            self.left = self.left.replace(self.order[self.level], "")
            self.level += 1

    parts = [Part(i) for i in range(len(PARTS))]
    before = len(link.made)
    for d in (2, 1, 3, 0):
        at = (link.z + d) % 4
        rows = pl.ds(pl.multiple_of(512 * at, 512), 512)
        value = jnp.dot(turned[rows], dz_ref[:, 0:384], preferred_element_type=F32)
        value = value.astype(BF16).reshape(4, 4, 32, 384)
        partial[0][at] = value[:, :, :, 0:256]
        partial[1][at] = value[:, :, :, 256:384]
        if d:
            parts[0].open((d,))
    parts[1].open((2,))
    for i in (2, 4):
        at, n = parts[i].at, parts[i].n + parts[i + 1].n
        value = jnp.dot(turned[...], dz_ref[:, at : at + n], preferred_element_type=F32)
        value = value.astype(BF16).reshape(4, 4, 4, 32, n)
        partial[i][...] = value[..., 0 : parts[i].n]
        partial[i + 1][...] = value[..., parts[i].n :]
        parts[i].open()
        parts[i + 1].open((2,))

    puts = []

    def features(i):
        rows = slice(1024 * i, 1024 * i + 1024)
        fgrads[:, rows] = dot_nt(dz_ref[0:256], weights[rows]).astype(BF16)
        for n, hbm in enumerate((qg_hbm, cg_hbm)):
            put = pltpu.make_async_copy(
                fgrads.at[pl.ds(128 * n, 128), pl.ds(1024 * i, 1024)],
                hbm.at[:, pl.ds(1024 * i, 1024)],
                local.at[4 + 2 * i + n],
            )
            put.start()
            puts.append(put)

    features(0)
    link.drain(before)
    for i in (0, 4, 2):
        parts[i].relay()
        parts[i + 1].open((1, 3))
        if i != 2:
            features(1 + i // 4)
    for i in (1, 5, 3):
        parts[i].relay()
    features(3)
    order = [parts[i] for i in (4, 0, 2, 5, 1, 3)]
    for level in range(3):
        link.drain(before)
        before = len(link.made)
        for part in order:
            part.close()
            if level < 2:
                part.open()
    for put in puts:
        put.wait()
    link.drain()


def place(q_in, c_in, p_in, q_out, c_out, p_out, q_held, c_held, p_held, come, leave):
    width = q_held.shape[1] // 4
    pairs = [(p_in, p_held, p_out)]
    for i in range(4):
        cols = pl.ds(width * i, width)
        pairs.append((q_in.at[:, cols], q_held.at[:, cols], q_out.at[:, cols]))
        pairs.append((c_in.at[:, cols], c_held.at[:, cols], c_out.at[:, cols]))
    first = [pltpu.make_async_copy(a, b, come.at[i]) for i, (a, b, _) in enumerate(pairs)]
    second = [pltpu.make_async_copy(b, c, leave.at[i]) for i, (_, b, c) in enumerate(pairs)]
    for copy in first:
        copy.start()
    for copy, onward in zip(first, second):
        copy.wait()
        onward.start()
    for copy in second:
        copy.wait()


def body(query_feat, code_feat, projection, hard_ids, loss_weight):
    rows, depth = query_feat.shape
    width = projection.shape[1]
    vmem = pl.BlockSpec(memory_space=pltpu.VMEM)
    anywhere = pl.BlockSpec(memory_space=pl.ANY)

    def vm(*shape, dtype=BF16):
        return pltpu.VMEM(shape, dtype)

    boxes = []
    for _, n, _ in PARTS:
        boxes += [vm(2, 4, 32, n)] * 2 + [vm(4, 4, 32, n)] * 3
        boxes += [vm(4, 32, n)] * 4 + [vm(32, n)] * 4
    outs = (
        jax.ShapeDtypeStruct((rows, depth), BF16),
        jax.ShapeDtypeStruct((rows, depth), BF16),
        jax.ShapeDtypeStruct((depth // 128, width), F32),
    )
    made = pl.pallas_call(
        step,
        out_shape=outs,
        in_specs=[anywhere] * 3 + [pl.BlockSpec(memory_space=pltpu.SMEM), vmem],
        out_specs=(anywhere, anywhere, vmem),
        scratch_shapes=[
            vm(256, depth),
            vm(8, 40, 128, dtype=F32),
            vm(32, 1024, dtype=F32),
            vm(depth, width),
            vm(256, depth),
            vm(256, depth // 2),
            vm(depth // 2, 512),
            vm(256, width, dtype=F32),
            vm(256, 1, dtype=F32),
            vm(512, width),
            vm(1024, width),
            vm(32, 64, width),
            vm(32, 64, 1024, dtype=F32),
            vm(2048, 1024),
            vm(256, 2048),
            vm(2048, width),
            vm(1024, width),
            vm(8, 40, 128, dtype=F32),
            vm(2, 8, 128, dtype=F32),
            vm(8, 128, dtype=F32),
            vm(8, 2, 8, 128, dtype=F32),
            vm(1, 1024, dtype=F32),
            vm(1, 1024, dtype=F32),
            vm(1, 1024, dtype=F32),
            vm(1, 1024, dtype=F32),
            vm(2, 128, width),
            vm(2, 128, width),
            vm(2, 256, width),
            vm(2, 256, width),
            vm(2, 32, width),
            vm(2, 32, width),
            vm(2, 64, width),
            vm(2, 64, width),
            vm(4, 128, width),
            vm(64, width),
            vm(64, width),
            vm(128, width),
            vm(128, width),
            vm(256, width),
            vm(256, width),
            vm(128, width, dtype=F32),
            *[vm(4, 4, 4, 32, n) for _, n, _ in PARTS],
            *boxes,
            pltpu.SemaphoreType.DMA((N_COPIES,)),
            pltpu.SemaphoreType.DMA((N_COPIES,)),
            pltpu.SemaphoreType.DMA((12,)),
        ],
        compiler_params=pltpu.CompilerParams(
            collective_id=0, has_side_effects=True, vmem_limit_bytes=60 * 2**20
        ),
        name="step",
    )(query_feat, code_feat, projection, hard_ids, loss_weight[None])
    return tuple(
        pl.pallas_call(
            place,
            out_shape=outs,
            in_specs=[anywhere] * 3,
            out_specs=(anywhere,) * 3,
            scratch_shapes=[
                vm(rows, depth),
                vm(rows, depth),
                vm(depth // 128, width, dtype=F32),
                pltpu.SemaphoreType.DMA((9,)),
                pltpu.SemaphoreType.DMA((9,)),
            ],
            name="place",
        )(*made)
    )


def solution(mesh):
    lined = P(("group", "member"), None)
    return jax.shard_map(
        body,
        mesh=mesh,
        in_specs=(lined, lined, P(), lined, P(("group", "member"))),
        out_specs=(lined, lined, lined),
        check_vma=False,
    )
```
